512 devices in a mesh: dp: 128 (over y, z, core), hg: 4 (over x).
Axes of the slice: x: 4, y: 4, z: 16, core: 2. Of those that a mesh axis runs over, the one named last changes fastest.
Arguments:
- queries: bfloat16 [128, 128, 576], P('dp', 'hg'), may hold values from -40 to 40
- latent_cache: bfloat16 [128, 512, 576], P('dp', 'hg'), may hold values from -8 to 8
- lengths: int32 [128], P('dp'), may hold values from 64 to 512, as said below
- residual: bfloat16 [2048, 3584], P('dp'), may hold values from -6 to 6
- partials: bfloat16 [4, 2048, 3584], P('hg', 'dp'), may hold values from -50 to 50
- norm_gain: float32 [3584], replicated, may hold values from 0.1 to 1.9
- router: bfloat16 [3584, 128], P(None, 'hg'), may hold values from -0.09375 to 0.09375
- expert_ids: int32 [2048, 8], P('dp'), may hold values from 0 to 127, all different within a row; in each aligned block of 16 rows (0 to 15, 16 to 31, ...) at most 2 rows name the same one
- up_proj: bfloat16 [128, 3584, 1024], P('dp', None, 'hg'), may hold values from -0.09375 to 0.09375
- down_proj: bfloat16 [128, 1024, 3584], P('dp', 'hg'), may hold values from -0.1875 to 0.1875
Outputs:
- attended: bfloat16 [128, 128, 512], P('dp', 'hg')
- layer_out: bfloat16 [2048, 3584], P('dp', 'hg')
The draws below stay inside these ranges and needn't reach their ends.
Inputs may be any that keep to these rules, and one draw needn't show every extreme that they name: `expert_ids`: each row names 8 different experts. Among the 16 rows of one dp index no expert is named more than 2 times, a bound that some block reaches. `lengths`: positions at or past a row's length are not attended. Some row has length 512 and some row has length 64.
All inputs are finite; a program needn't handle non-finite values.
Results may differ from the reference program's by a relative error of at most 0.015.
Values may be sent and summed in bfloat16 or wider, within the bound.
No kernel may reach another device: no remote copies, remote signals or barrier semaphores. Data moves between devices by JAX's collectives and lax.ppermute only.
A program may use at most 64 MiB of HBM per device.

```python
import math
import jax
import jax.numpy as jnp
import numpy as np
from jax import lax

D = 3584
FF = 1024
HEADS = 128
LATENT = 512
TOPK = 8
ROWS_B = 16
LENGTH = 512
KV = 576
GROUPS = 4
FF_DEV = 256
EXPERTS = 128
CAP = 2
TOKENS_B = 2048
ATT_ROWS = 128
N_DP = 128
N_HG = 4


def draw_queries(key, part):
    key = jax.random.fold_in(key, 11)
    base = 1.2 * jax.random.normal(key, (ATT_ROWS, HEADS, KV), jnp.float32)
    return base.astype(jnp.bfloat16)


def draw_latent_cache(key, part):
    key = jax.random.fold_in(key, 13)
    base = jax.random.normal(key, (ATT_ROWS, LENGTH, KV), jnp.float32)
    return base.astype(jnp.bfloat16)


def draw_lengths(key, part):
    key = jax.random.fold_in(key, 7)
    first_key, second_key, third_key = jax.random.split(key, 3)
    drawn = jax.random.randint(first_key, (ATT_ROWS,), LENGTH // 8, LENGTH + 1, dtype=jnp.int32)
    longest = jax.random.randint(second_key, (), 0, ATT_ROWS, dtype=jnp.int32)
    stride = jax.random.randint(third_key, (), 1, ATT_ROWS, dtype=jnp.int32)
    shortest = (longest + stride) % ATT_ROWS
    return drawn.at[longest].set(LENGTH).at[shortest].set(LENGTH // 8)


def draw_partials(key, part):
    key = jax.random.fold_in(key, 5)
    key_own = jax.random.fold_in(key, 0)
    own = jax.random.normal(key_own, (GROUPS, TOKENS_B, D), jnp.float32)
    own = 0.5 * jnp.clip(own, -6.0, 6.0)
    return own.astype(jnp.bfloat16)


def level_of(key, extent, cuts, smallest, high):
    factor_of, own = 1.0, jax.random.fold_in(key, 6)
    for dim, blocks in cuts:
        heights = jnp.exp(jax.random.uniform(jax.random.fold_in(own, dim), (blocks,), jnp.float32, smallest / len(cuts), high / len(cuts)))
        factor_of = factor_of * jnp.repeat(heights, extent[dim] // blocks).reshape([-1 if axis == dim else 1 for axis in range(len(extent))])
    return factor_of


def assign_block(rng, own, number, rows, amount, top, most, lean):
    order = jax.random.permutation(rng, amount)
    heavy_load, ordinary = portions_of(amount, rows * top, most, lean, True), portions_of(amount, rows * top, most, lean, False)
    places = jnp.arange(amount)

    def named(sizes, turn):
        used = int((sizes > 0).sum())
        fixed = max(1, used // 4)
        shifted = fixed + (places - fixed + turn * (used - fixed)) % max(1, amount - fixed)
        return jnp.zeros((amount,), jnp.int32).at[order[jnp.where(places < fixed, places, shifted)]].set(jnp.asarray(sizes, jnp.int32))

    sizes = jnp.where(number % 4 == 0, named(heavy_load, number // 4), named(ordinary, number - number // 4 - 1))
    mixed = jax.random.permutation(jax.random.fold_in(own, 3), amount)
    donor, taker = mixed[0:amount // 2 * 2:2], mixed[1:amount // 2 * 2:2]
    room = jnp.minimum(sizes[donor] - 1, most - sizes[taker]) // 2
    room = jnp.where((donor == order[0]) | (taker == order[0]) | (sizes[taker] == 0), 0, jnp.maximum(room, 0))
    shifted = jax.random.randint(jax.random.fold_in(own, 4), (amount // 2,), 0, 1 << 20) % (room + 1)
    sizes = sizes.at[donor].add(-shifted).at[taker].add(shifted)
    labels = jnp.searchsorted(jnp.cumsum(sizes), jnp.arange(rows * top), side="right").astype(jnp.int32)
    listing = labels.reshape(top, rows).T
    listing = listing[jax.random.permutation(jax.random.fold_in(own, 1), rows)]
    turn = jax.random.randint(jax.random.fold_in(own, 2), (rows, 1), 0, top)
    return jnp.take_along_axis(listing, (jnp.arange(top)[None, :] + turn) % top, axis=1)


def portions_of(count, total, limit, lean, full):
    portions = [(1 << 20) // math.isqrt(standing ** lean) + 1 for standing in range(1, count + 1)]
    largest = limit if full else min(limit, max(-(-total // count), total * portions[0] // sum(portions)))
    least = 1 if total - largest >= count - 1 else 0
    counts, rest = [largest] + [least] * (count - 1), total - largest - least * (count - 1)
    while rest > 0:
        free = [i for i in range(1, count) if counts[i] < largest] or [i for i in range(1, count) if counts[i] < limit]
        mass, remaining = sum([portions[i] for i in free]), rest
        for i in free:
            more = min(limit - counts[i], max(1, remaining * portions[i] // mass), rest)
            counts[i] = counts[i] + more
            rest = rest - more
    return np.array(counts)


def normal_values(key, dims, deviation, reach, shards=(), held_as=jnp.bfloat16):
    values = deviation * jax.random.normal(key, dims, jnp.float32)
    if shards:
        values = values * level_of(key, dims, shards, -0.22, 0.18)
    return jnp.clip(values, -reach, reach).astype(held_as)


def setup_inputs(seed: int = 0) -> dict:
    splits = jax.random.split(jax.random.key(seed), 11)
    queries = draw_queries(jax.random.fold_in(splits[10], 71), 0)
    latent_cache = draw_latent_cache(jax.random.fold_in(splits[10], 71), 0)
    lengths = draw_lengths(jax.random.fold_in(splits[10], 71), 0)
    residual = normal_values(splits[3], (TOKENS_B, D), 1.0, 6.0, ((0, 128),))
    partials = draw_partials(jax.random.fold_in(splits[10], 71), 0)
    norm_gain = jnp.clip(1.0 + 0.18 * jax.random.normal(splits[5], (D,), jnp.float32), 0.1, 1.9)
    router = normal_values(splits[6], (D, EXPERTS), D ** -0.5, 0.09375, ((1, 4),))
    expert_ids_keys = jax.random.split(jax.random.fold_in(splits[7], 1), TOKENS_B // ROWS_B)
    expert_ids_turns = jax.random.permutation(jax.random.fold_in(splits[7], 3), TOKENS_B // ROWS_B)
    expert_ids = jax.vmap(lambda own, number: assign_block(jax.random.fold_in(splits[7], 2), own, number, ROWS_B, EXPERTS, TOPK, CAP, 2))(expert_ids_keys, expert_ids_turns).reshape((TOKENS_B, TOPK))
    up_proj = normal_values(splits[8], (EXPERTS, D, FF), D ** -0.5, 0.09375, ((0, 128), (2, 4)))
    down_proj = normal_values(splits[9], (EXPERTS, FF, D), FF ** -0.5, 0.1875, ((0, 128), (1, 4)))
    return dict(queries=queries, latent_cache=latent_cache, lengths=lengths, residual=residual, partials=partials, norm_gain=norm_gain, router=router, expert_ids=expert_ids, up_proj=up_proj, down_proj=down_proj)


SOFTMAX_SCALE = 192.0 ** (-0.5)
ROUTE_SCALE = 2.5
NORM_EPS = 1e-06

def attend_row(packed):
    query_row, cache_row, length_row = packed
    scores = jnp.dot(query_row, cache_row.T, preferred_element_type=jnp.float32) * SOFTMAX_SCALE
    in_range = jnp.arange(LENGTH, dtype=jnp.int32) < length_row
    scores = jnp.where(in_range[None, :], scores, -jnp.inf)
    largest = lax.optimization_barrier(jnp.max(scores, axis=1, keepdims=True))
    weights = jnp.exp(scores - largest)
    probabilities = (weights / lax.optimization_barrier(jnp.sum(weights, axis=1, keepdims=True))).astype(jnp.bfloat16)
    combined = jnp.dot(probabilities, cache_row[:, :LATENT], preferred_element_type=jnp.float32)
    return combined.astype(jnp.bfloat16)

def capacity_slots(expert_ids):
    blocks = expert_ids.reshape(N_DP, ROWS_B * TOPK)
    numbers = jnp.arange(EXPERTS, dtype=jnp.int32)
    onehot = (blocks[:, :, None] == numbers[None, None, :]).astype(jnp.int32)
    before = jnp.cumsum(onehot, axis=1) - onehot
    return lax.optimization_barrier(jnp.sum(before * onehot, axis=2)).reshape(TOKENS_B, TOPK)

def reference(queries, latent_cache, lengths, residual, partials, norm_gain, router, expert_ids, up_proj, down_proj):
    attended = lax.map(attend_row, (queries, latent_cache, lengths))
    hidden = residual.astype(jnp.float32) + lax.optimization_barrier(jnp.sum(partials.astype(jnp.float32), axis=0))
    mean_square = lax.optimization_barrier(jnp.mean(hidden * hidden, axis=1, keepdims=True))
    normed = (hidden * lax.rsqrt(mean_square + NORM_EPS) * norm_gain).astype(jnp.bfloat16)
    logits = jnp.dot(normed, router, preferred_element_type=jnp.float32)
    chosen = jnp.take_along_axis(logits, expert_ids, axis=1)
    affinity = jax.nn.sigmoid(chosen)
    gate_values = (ROUTE_SCALE * affinity / lax.optimization_barrier(jnp.sum(affinity, axis=1, keepdims=True))).astype(jnp.bfloat16)
    slot_index = capacity_slots(expert_ids)
    source = (jnp.arange(TOKENS_B, dtype=jnp.int32) // ROWS_B)[:, None]
    places = ((expert_ids * N_DP + source) * CAP + slot_index).reshape(-1).astype(jnp.int32)
    owners = jnp.repeat(jnp.arange(TOKENS_B, dtype=jnp.int32), TOPK)
    slot_count = N_DP * CAP
    token_table = jnp.full((EXPERTS * slot_count,), TOKENS_B, jnp.int32).at[places].set(owners)
    gate_table = jnp.zeros((EXPERTS * slot_count,), jnp.float32).at[places].set(gate_values.reshape(-1).astype(jnp.float32))
    padded = jnp.concatenate([normed, jnp.zeros((1, D), jnp.bfloat16)], axis=0)

    def expert_step(accumulated, expert):
        first_slot = (expert * slot_count).astype(jnp.int32)
        token_rows = lax.dynamic_slice_in_dim(token_table, first_slot, slot_count)
        gate_rows = lax.dynamic_slice_in_dim(gate_table, first_slot, slot_count)
        inputs = padded[token_rows]
        activated = jax.nn.silu(jnp.dot(inputs, up_proj[expert], preferred_element_type=jnp.float32)).astype(jnp.bfloat16)
        weight_down = down_proj[expert]
        summed = jnp.zeros((slot_count, D), jnp.float32)
        for group_index in range(N_HG):
            first_unit = group_index * FF_DEV
            group_part = jnp.dot(activated[:, first_unit:first_unit + FF_DEV], weight_down[first_unit:first_unit + FF_DEV], preferred_element_type=jnp.float32)
            rounded = lax.optimization_barrier(group_part.astype(jnp.bfloat16))
            summed = summed + rounded.astype(jnp.float32)
        return (accumulated.at[token_rows].add(gate_rows[:, None] * summed), None)
    start_sum = jnp.zeros((TOKENS_B + 1, D), jnp.float32)
    routed_sum, unused_out = lax.scan(expert_step, start_sum, jnp.arange(EXPERTS, dtype=jnp.int32))
    layer_out = (hidden + routed_sum[:TOKENS_B]).astype(jnp.bfloat16)
    return (attended, layer_out)
```

```python
import jax
import jax.numpy as jnp
from jax import lax
from jax.experimental import pallas as pl
from jax.experimental.pallas import tpu as pltpu
from jax.sharding import PartitionSpec as P

LATENT = 512
SOFTMAX_SCALE = 192.0 ** (-0.5)
ROUTE_SCALE = 2.5
NORM_EPS = 1e-06


def shift(value, distance, size):
    return lax.ppermute(value, "hg", [(i, (i + distance) % size) for i in range(size)])


def spread(value, size):
    return lax.all_to_all(jnp.broadcast_to(value[None], (size,) + value.shape), "hg", 0, 0, tiled=True)


def spread_ready(value):
    return lax.all_to_all(value, "hg", 0, 0, tiled=True)


def attention(queries, latent_cache, lengths):
    size = lax.axis_size("hg")
    me = lax.axis_index("hg")
    width = latent_cache.shape[1]
    blocks = [latent_cache] + [shift(latent_cache, d, size) for d in range(1, size)]
    whole_cache = jnp.concatenate(blocks, axis=1)
    places = jnp.arange(size * width, dtype=jnp.int32)
    owner = (me - places // width + size) % size
    positions = owner * width + places % width
    scores = (
        jnp.einsum("rhc,rpc->rhp", queries, whole_cache, preferred_element_type=jnp.float32)
        * SOFTMAX_SCALE
    )
    in_range = positions[None, :] < lengths[:, None]
    scores = jnp.where(in_range[:, None, :], scores, -jnp.inf)
    largest = jnp.max(scores, axis=2, keepdims=True)
    weights = jnp.exp(scores - largest)
    probabilities = (weights / jnp.sum(weights, axis=2, keepdims=True)).astype(jnp.bfloat16)
    combined = jnp.einsum(
        "rhp,rpc->rhc",
        probabilities,
        whole_cache[:, :, :LATENT],
        preferred_element_type=jnp.float32,
    )
    return combined.astype(jnp.bfloat16)


def column_blocks(weights, size):
    depth, width = weights.shape
    part = width // size

    def kernel(weights_ref, *outs):
        me = lax.axis_index("hg")
        for d in range(size):
            start = pl.multiple_of(lax.rem(me + d, size) * part, 128)
            outs[d][...] = weights_ref[:, pl.ds(start, part)]

    return pl.pallas_call(
        kernel,
        out_shape=[jax.ShapeDtypeStruct((depth, part), weights.dtype)] * size,
        cost_estimate=pl.CostEstimate(flops=0, bytes_accessed=4 * depth * width, transcendentals=0),
        compiler_params=pltpu.CompilerParams(vmem_limit_bytes=20 << 20),
        name="column_blocks",
    )(weights)


def expert_up(all_rows, weights, extra):
    size, slots, part = all_rows.shape
    units = weights.shape[1]
    more = extra.shape[0]

    def kernel(rows_ref, weights_ref, extra_ref, out_ref):
        total = jnp.zeros((slots, units), jnp.float32)
        for x in range(size):
            total += jnp.dot(
                rows_ref[x], weights_ref[x * part:(x + 1) * part, :],
                preferred_element_type=jnp.float32,
            )
        active = (total / (1.0 + jnp.exp(-total))).astype(jnp.bfloat16)
        for x in range(size):
            out_ref[x, :slots, :] = active
            out_ref[x, slots:, :] = extra_ref[...]

    return pl.pallas_call(
        kernel,
        out_shape=jax.ShapeDtypeStruct((size, slots + more, units), jnp.bfloat16),
        cost_estimate=pl.CostEstimate(
            flops=2 * slots * size * part * units,
            bytes_accessed=2 * (slots * size * part + size * part * units + size * slots * units),
            transcendentals=slots * units,
        ),
        compiler_params=pltpu.CompilerParams(vmem_limit_bytes=40 << 20),
        name="expert_up",
    )(all_rows, weights, extra)


def expert_down(active, blocks, slots):
    size, _, units = active.shape
    part = blocks[0].shape[1]

    def kernel(active_ref, *rest):
        blocks_ref, out_ref = rest[:size], rest[size]
        me = lax.axis_index("hg")
        total = jnp.zeros((slots, part), jnp.float32)
        for d in range(size):
            owner = lax.rem(me + size - d, size)
            total += jnp.dot(
                active_ref[owner, :slots, :], blocks_ref[d][...],
                preferred_element_type=jnp.float32,
            )
        out_ref[...] = total.astype(jnp.bfloat16)

    return pl.pallas_call(
        kernel,
        out_shape=jax.ShapeDtypeStruct((slots, part), jnp.bfloat16),
        cost_estimate=pl.CostEstimate(
            flops=2 * slots * size * part * units,
            bytes_accessed=2 * (slots * size * units + size * part * units + slots * part),
            transcendentals=0,
        ),
        compiler_params=pltpu.CompilerParams(vmem_limit_bytes=40 << 20),
        name="expert_down",
    )(active, *blocks)


def on_device(
    queries,
    latent_cache,
    lengths,
    residual,
    partials,
    norm_gain,
    router,
    expert_ids,
    up_proj,
    down_proj,
):
    size = lax.axis_size("hg")
    me = lax.axis_index("hg")
    row_count, feature_width = residual.shape
    top_count = expert_ids.shape[1]
    experts = lax.axis_size("dp") * up_proj.shape[0]
    capacity = min(row_count, max(2, 2 * row_count * top_count // experts))
    slice_width = feature_width // size
    unit_count = up_proj.shape[2]

    attended = attention(queries, latent_cache, lengths)

    hidden = residual.astype(jnp.float32) + jnp.sum(
        spread(partials[0], size).astype(jnp.float32), axis=0
    )
    mean_square = jnp.mean(hidden * hidden, axis=1, keepdims=True)
    normed = (hidden * lax.rsqrt(mean_square + NORM_EPS) * norm_gain).astype(jnp.bfloat16)

    numbers = jnp.arange(experts, dtype=jnp.int32)
    flat_ids = expert_ids.reshape(-1)
    onehot = (flat_ids[:, None] == numbers[None, :]).astype(jnp.int32)
    slot_index = jnp.sum((jnp.cumsum(onehot, axis=0) - onehot) * onehot, axis=1).reshape(
        row_count, top_count
    )
    target = expert_ids * capacity + slot_index
    slot_lanes = jnp.arange(experts * capacity, dtype=jnp.int32)
    slot_hits = target[:, :, None] == slot_lanes[None, None, :]
    route_matrix = jnp.any(slot_hits, axis=1).astype(jnp.bfloat16)

    normed_slice = lax.dynamic_slice_in_dim(normed, me * slice_width, slice_width, 1)
    outgoing = jnp.einsum(
        "te,td->ed", route_matrix, normed_slice, preferred_element_type=jnp.float32
    ).astype(jnp.bfloat16)
    outgoing = outgoing.reshape(experts, capacity, slice_width)
    down_own, *down_sent = column_blocks(down_proj[0], size)
    outgoing, *down_sent = lax.optimization_barrier((outgoing, *down_sent))
    arrived = lax.all_to_all(outgoing, "dp", split_axis=0, concat_axis=0, tiled=True)
    down_got = [shift(block, d + 1, size) for d, block in enumerate(down_sent)]
    local_logits = jnp.dot(normed, router, preferred_element_type=jnp.float32)
    high = local_logits.astype(jnp.bfloat16)
    low = (local_logits - high.astype(jnp.float32)).astype(jnp.bfloat16)
    local = experts // size
    extra = jnp.pad(
        jnp.concatenate([high, low], axis=1), ((0, 0), (0, unit_count - 2 * local))
    )
    arrived, extra, *down_got = lax.optimization_barrier((arrived, extra, *down_got))
    slots = experts * capacity
    rows = arrived.reshape(slots, slice_width)

    active = spread_ready(expert_up(spread(rows, size), up_proj[0], extra))
    reduced = expert_down(active, [down_own, *down_got], slots)
    returned = lax.all_to_all(
        reduced.reshape(experts, capacity, slice_width),
        "dp", split_axis=0, concat_axis=0, tiled=True,
    ).reshape(slots, slice_width)

    logit_parts = active[:, slots:, :2 * local].astype(jnp.float32)
    logits = (logit_parts[:, :, :local] + logit_parts[:, :, local:]).transpose(1, 0, 2).reshape(
        row_count, experts
    )
    picker = expert_ids[:, :, None] == numbers[None, None, :]
    chosen = jnp.sum(jnp.where(picker, logits[:, None, :], 0.0), axis=2)
    affinity = jax.nn.sigmoid(chosen)
    gate_values = (ROUTE_SCALE * affinity / jnp.sum(affinity, axis=1, keepdims=True)).astype(
        jnp.bfloat16
    )
    gate_matrix = jnp.sum(
        jnp.where(slot_hits, gate_values[:, :, None].astype(jnp.float32), 0.0), axis=1
    ).astype(jnp.bfloat16)
    routed_sum = jnp.dot(gate_matrix, returned, preferred_element_type=jnp.float32)
    hidden_slice = lax.dynamic_slice_in_dim(hidden, me * slice_width, slice_width, 1)
    layer_out = (hidden_slice + routed_sum).astype(jnp.bfloat16)
    return (attended, layer_out)


def solution(mesh):
    return jax.shard_map(
        on_device,
        mesh=mesh,
        in_specs=(
            P("dp", "hg", None),
            P("dp", "hg", None),
            P("dp"),
            P("dp", None),
            P("hg", "dp", None),
            P(),
            P(None, "hg"),
            P("dp", None),
            P("dp", None, "hg"),
            P("dp", "hg", None),
        ),
        out_specs=(P("dp", "hg", None), P("dp", "hg")),
        check_vma=False,
    )
```

```python
import jax
import jax.numpy as jnp
from jax import lax
from jax.experimental import pallas as pl
from jax.experimental.pallas import tpu as pltpu
from jax.sharding import PartitionSpec as P

LATENT = 512
SOFTMAX_SCALE = 192.0 ** (-0.5)
ROUTE_SCALE = 2.5
NORM_EPS = 1e-06
VMEM_LIMIT = 16 << 20
WHOLE_VMEM = 60 << 20


def shift(value, distance, size):
    return lax.ppermute(value, "hg", [(i, (i + distance) % size) for i in range(size)])


def spread(value, size):
    return lax.all_to_all(jnp.broadcast_to(value[None], (size,) + value.shape), "hg", 0, 0, tiled=True)


def exchange(value):
    return lax.all_to_all(value, "hg", 0, 0, tiled=True)


def attention(queries, latent_cache, lengths):
    size = lax.axis_size("hg")
    me = lax.axis_index("hg")
    width = latent_cache.shape[1]
    blocks = [latent_cache] + [shift(latent_cache, d, size) for d in range(1, size)]
    whole_cache = jnp.concatenate(blocks, axis=1)
    places = jnp.arange(size * width, dtype=jnp.int32)
    owner = (me - places // width + size) % size
    positions = owner * width + places % width
    scores = (
        jnp.einsum("rhc,rpc->rhp", queries, whole_cache, preferred_element_type=jnp.float32)
        * SOFTMAX_SCALE
    )
    in_range = positions[None, :] < lengths[:, None]
    scores = jnp.where(in_range[:, None, :], scores, -jnp.inf)
    largest = jnp.max(scores, axis=2, keepdims=True)
    weights = jnp.exp(scores - largest)
    probabilities = (weights / jnp.sum(weights, axis=2, keepdims=True)).astype(jnp.bfloat16)
    combined = jnp.einsum(
        "rhp,rpc->rhc",
        probabilities,
        whole_cache[:, :, :LATENT],
        preferred_element_type=jnp.float32,
    )
    return combined.astype(jnp.bfloat16)


HBM = pl.BlockSpec(memory_space=pltpu.HBM)
VMEM = pl.BlockSpec(memory_space=pltpu.VMEM)


def start_all(pairs, sems, first=0):
    copies = [
        pltpu.make_async_copy(source, target, sems.at[first + i])
        for i, (source, target) in enumerate(pairs)
    ]
    for copy in copies:
        copy.start()
    return copies


def wait_all(copies):
    for copy in copies:
        copy.wait()


def place(d, size, width):
    return pl.multiple_of(lax.rem(lax.axis_index("hg") + d, size) * width, 128)


def pack_weights(up_weights, down_weights, earlier, size):
    features, units = up_weights.shape
    part = features // size
    half = units // 2
    chunks = part // 128
    block = 2 * part
    assert units == 256 and size == 4 and part % 128 == 0 and block == chunks * units
    turns = (1, 3, 2)

    def kernel(up_hbm, down_hbm, earlier_ref, next_hbm, back_hbm, up_ref, down_ref, next_ref, back_ref, sems):
        ups = start_all(
            [(up_hbm.at[pl.ds(place(d, size, part), part), :], up_ref.at[i]) for i, d in enumerate(turns)], sems
        )
        downs = start_all(
            [(down_hbm.at[:, pl.ds(place(d, size, part), part)], down_ref.at[i]) for i, d in enumerate(turns)], sems, 3
        )
        outs = []
        for i, (to_ref, to_hbm) in enumerate(((next_ref, next_hbm), (back_ref, back_hbm))):
            ups[i].wait()
            to_ref[:part, :] = up_ref[i, :, :half]
            to_ref[part:block, :] = up_ref[i, :, half:]
            downs[i].wait()
            for k in range(chunks):
                to_ref[block + k * units:block + (k + 1) * units, :] = down_ref[i, :, k * 128:(k + 1) * 128]
            outs += start_all(
                [(to_ref.at[:2 * block, :], to_hbm.at[:2 * block, :])], sems, 6 + 2 * i
            )
        ups[2].wait()
        downs[2].wait()
        for i, (to_ref, to_hbm) in enumerate(((next_ref, next_hbm), (back_ref, back_hbm))):
            first = 2 * block
            to_ref[first:first + part, :] = up_ref[2, :, i * half:(i + 1) * half]
            first += part
            for k in range(chunks):
                to_ref[first + k * half:first + (k + 1) * half, :] = down_ref[
                    2, i * half:(i + 1) * half, k * 128:(k + 1) * 128
                ]
            outs += start_all(
                [(to_ref.at[2 * block:, :], to_hbm.at[2 * block:, :])], sems, 7 + 2 * i
            )
        wait_all(outs)

    sent = pltpu.HBM((3 * block, 128), up_weights.dtype)
    return pl.pallas_call(
        kernel,
        out_shape=[sent, sent],
        in_specs=[HBM, HBM, pl.BlockSpec(memory_space=pl.ANY)],
        out_specs=[HBM, HBM],
        scratch_shapes=[
            pltpu.VMEM((3, part, units), up_weights.dtype),
            pltpu.VMEM((3, units, part), up_weights.dtype),
            pltpu.VMEM((3 * block, 128), up_weights.dtype),
            pltpu.VMEM((3 * block, 128), up_weights.dtype),
            pltpu.SemaphoreType.DMA((10,)),
        ],
        cost_estimate=pl.CostEstimate(
            flops=0, bytes_accessed=8 * features * units, transcendentals=0
        ),
        compiler_params=pltpu.CompilerParams(vmem_limit_bytes=WHOLE_VMEM),
        name="pack_weights",
    )(up_weights, down_weights, earlier)


def own_blocks(up_weights, down_weights, earlier, size):
    features, units = up_weights.shape
    part = features // size

    def kernel(up_hbm, down_hbm, earlier_ref, own_up_hbm, own_down_hbm, up_ref, down_ref, sems):
        wait_all(start_all(
            [
                (up_hbm.at[pl.ds(place(0, size, part), part), :], up_ref),
                (down_hbm.at[:, pl.ds(place(0, size, part), part)], down_ref),
            ],
            sems,
        ))
        wait_all(start_all([(up_ref, own_up_hbm), (down_ref, own_down_hbm)], sems, 2))

    dtype = up_weights.dtype
    return pl.pallas_call(
        kernel,
        out_shape=[pltpu.HBM((part, units), dtype), pltpu.HBM((units, part), dtype)],
        in_specs=[HBM, HBM, pl.BlockSpec(memory_space=pl.ANY)],
        out_specs=[HBM, HBM],
        scratch_shapes=[
            pltpu.VMEM((part, units), dtype),
            pltpu.VMEM((units, part), dtype),
            pltpu.SemaphoreType.DMA((4,)),
        ],
        compiler_params=pltpu.CompilerParams(vmem_limit_bytes=WHOLE_VMEM),
        name="own_blocks",
    )(up_weights, down_weights, earlier)


def join_weights(own_up, own_down, after, before, far_low, far_high):
    part, units = own_up.shape
    half = units // 2
    chunks = part // 128
    block = 2 * part

    def kernel(own_up_ref, own_down_ref, after_ref, before_ref, low_ref, high_ref, up_ref, down_ref):
        up_ref[:, :units] = own_up_ref[...]
        up_ref[:, units:units + half] = after_ref[:part, :]
        up_ref[:, units + half:2 * units] = after_ref[part:block, :]
        up_ref[:, 2 * units:2 * units + half] = low_ref[:part, :]
        up_ref[:, 2 * units + half:3 * units] = high_ref[:part, :]
        up_ref[:, 3 * units:3 * units + half] = before_ref[:part, :]
        up_ref[:, 3 * units + half:] = before_ref[part:block, :]
        down_ref[:units, :] = own_down_ref[...]
        for k in range(chunks):
            lanes = slice(k * 128, (k + 1) * 128)
            whole = slice(block + k * units, block + (k + 1) * units)
            some = slice(part + k * half, part + (k + 1) * half)
            down_ref[units:2 * units, lanes] = after_ref[whole, :]
            down_ref[2 * units:2 * units + half, lanes] = low_ref[some, :]
            down_ref[2 * units + half:3 * units, lanes] = high_ref[some, :]
            down_ref[3 * units:, lanes] = before_ref[whole, :]

    return pl.pallas_call(
        kernel,
        out_shape=[
            jax.ShapeDtypeStruct((part, 4 * units), own_up.dtype),
            jax.ShapeDtypeStruct((4 * units, part), own_up.dtype),
        ],
        cost_estimate=pl.CostEstimate(
            flops=0, bytes_accessed=32 * part * units, transcendentals=0
        ),
        compiler_params=pltpu.CompilerParams(vmem_limit_bytes=VMEM_LIMIT),
        name="join_weights",
    )(own_up, own_down, after, before, far_low, far_high)


def norm_and_route(copies, residual, gain, choices, experts, capacity):
    size, rows, features = copies.shape
    part = features // size
    slots = experts * capacity
    top = choices.shape[0]

    def kernel(
        copies_ref, residual_hbm, gain_hbm, choices_hbm, normed_hbm, hidden_hbm, route_hbm, out_hbm,
        residual_ref, gain_ref, choices_ref, hidden_ref, normed_ref, route_ref, out_ref, sems,
    ):
        fetched = start_all(
            [(choices_hbm, choices_ref), (residual_hbm, residual_ref), (gain_hbm, gain_ref)], sems, 4
        )
        fetched[0].wait()
        expert = lax.div(lax.broadcasted_iota(jnp.int32, (slots, rows), 0), capacity)
        slot = lax.broadcasted_iota(jnp.int32, (slots, rows), 0) - expert * capacity
        hits = jnp.zeros((slots, rows), jnp.float32)
        for k in range(top):
            hits += jnp.where(choices_ref[k:k + 1, :] == expert, 1.0, 0.0)
        above = lax.broadcasted_iota(jnp.int32, (rows, rows), 0) < lax.broadcasted_iota(
            jnp.int32, (rows, rows), 1
        )
        earlier = jnp.dot(
            hits.astype(jnp.bfloat16), jnp.where(above, 1.0, 0.0).astype(jnp.bfloat16),
            preferred_element_type=jnp.float32,
        )
        route = jnp.where(earlier == slot.astype(jnp.float32), hits, 0.0).astype(jnp.bfloat16)
        route_ref[...] = route

        wait_all(fetched[1:])
        hidden = residual_ref[...].astype(jnp.float32)
        for x in range(size):
            hidden += copies_ref[x].astype(jnp.float32)
        hidden_ref[...] = hidden
        scale = lax.rsqrt(jnp.mean(hidden * hidden, axis=1, keepdims=True) + NORM_EPS)
        normed_ref[...] = (hidden * scale * gain_ref[...][None, :]).astype(jnp.bfloat16)
        mine = pl.ds(place(0, size, part), part)
        out_ref[...] = jnp.dot(
            route, normed_ref[:, mine], preferred_element_type=jnp.float32
        ).astype(jnp.bfloat16).reshape(experts, capacity, part)
        wait_all(start_all(
            [
                (out_ref, out_hbm),
                (normed_ref, normed_hbm),
                (hidden_ref.at[:, mine], hidden_hbm),
                (route_ref, route_hbm),
            ],
            sems,
        ))

    shapes = [
        ((rows, features), jnp.bfloat16),
        ((rows, part), jnp.float32),
        ((slots, rows), jnp.bfloat16),
        ((experts, capacity, part), jnp.bfloat16),
    ]
    return pl.pallas_call(
        kernel,
        out_shape=[pltpu.HBM(*shape) for shape in shapes],
        in_specs=[VMEM, HBM, HBM, HBM],
        out_specs=[HBM] * 4,
        scratch_shapes=[
            pltpu.VMEM(residual.shape, residual.dtype),
            pltpu.VMEM(gain.shape, gain.dtype),
            pltpu.VMEM(choices.shape, choices.dtype),
            pltpu.VMEM((rows, features), jnp.float32),
            pltpu.VMEM((rows, features), jnp.bfloat16),
            pltpu.VMEM((slots, rows), jnp.bfloat16),
            pltpu.VMEM((experts, capacity, part), jnp.bfloat16),
            pltpu.SemaphoreType.DMA((7,)),
        ],
        cost_estimate=pl.CostEstimate(
            flops=2 * slots * rows * part,
            bytes_accessed=2 * (size + 2) * rows * features + 2 * slots * part,
            transcendentals=0,
        ),
        compiler_params=pltpu.CompilerParams(vmem_limit_bytes=VMEM_LIMIT),
        name="norm_and_route",
    )(copies, residual, gain, choices)


def gates(logit_parts, route, experts, capacity):
    size, rows, lanes = logit_parts.shape
    slots = experts * capacity
    local = experts // size

    def kernel(parts_ref, route_ref, out_ref):
        expert = lax.div(lax.broadcasted_iota(jnp.int32, (slots, lanes), 0), capacity)
        lane = lax.broadcasted_iota(jnp.int32, (slots, lanes), 1)
        column = jnp.where(lane < local, lane, lane - local)
        logits = jnp.zeros((slots, rows), jnp.float32)
        for x in range(size):
            pick = (column + x * local == expert) & (lane < 2 * local)
            logits += lax.dot_general(
                jnp.where(pick, 1.0, 0.0).astype(jnp.bfloat16), parts_ref[x],
                (((1,), (1,)), ((), ())), preferred_element_type=jnp.float32,
            )
        affinity = route_ref[...].astype(jnp.float32) / (1.0 + jnp.exp(-logits))
        total = jnp.sum(affinity, axis=0, keepdims=True)
        out_ref[...] = (ROUTE_SCALE * affinity / total).astype(jnp.bfloat16)

    return pl.pallas_call(
        kernel,
        out_shape=jax.ShapeDtypeStruct((slots, rows), jnp.bfloat16),
        name="gates",
    )(logit_parts, route)


def combine(gate_matrix, returned, hidden):
    experts, capacity, part = returned.shape
    slots = experts * capacity

    def kernel(gates_hbm, returned_ref, hidden_hbm, out_ref, gates_ref, hidden_ref, sems):
        copies = start_all([(gates_hbm, gates_ref), (hidden_hbm, hidden_ref)], sems)
        wait_all(copies)
        routed = lax.dot_general(
            gates_ref[...], returned_ref[...].reshape(slots, part), (((0,), (0,)), ((), ())),
            preferred_element_type=jnp.float32,
        )
        out_ref[...] = (hidden_ref[...] + routed).astype(jnp.bfloat16)

    return pl.pallas_call(
        kernel,
        out_shape=jax.ShapeDtypeStruct(hidden.shape, jnp.bfloat16),
        in_specs=[HBM, VMEM, HBM],
        scratch_shapes=[
            pltpu.VMEM(gate_matrix.shape, gate_matrix.dtype),
            pltpu.VMEM(hidden.shape, hidden.dtype),
            pltpu.SemaphoreType.DMA((2,)),
        ],
        compiler_params=pltpu.CompilerParams(vmem_limit_bytes=VMEM_LIMIT),
        name="combine",
    )(gate_matrix, returned, hidden)


def expert_up(arrived, weights):
    size = lax.axis_size("hg")
    experts, capacity, part = arrived.shape
    slots = experts * capacity
    units = weights.shape[1] // size

    def kernel(rows_ref, weights_ref, out_ref):
        me = lax.axis_index("hg")
        rows = rows_ref[...].reshape(slots, part)
        for d in range(size):
            owner = lax.rem(me + size - d, size)
            out_ref[owner] = jnp.dot(
                rows, weights_ref[:, d * units:(d + 1) * units],
                preferred_element_type=jnp.float32,
            ).astype(jnp.bfloat16)

    return pl.pallas_call(
        kernel,
        out_shape=jax.ShapeDtypeStruct((size, slots, units), jnp.bfloat16),
        cost_estimate=pl.CostEstimate(
            flops=2 * slots * size * part * units,
            bytes_accessed=2 * (slots * part + size * part * units + size * slots * units),
            transcendentals=0,
        ),
        compiler_params=pltpu.CompilerParams(vmem_limit_bytes=VMEM_LIMIT),
        name="expert_up",
    )(arrived, weights)


def expert_silu(shares, extra):
    size, slots, units = shares.shape
    more = extra.shape[0]

    def kernel(shares_hbm, extra_hbm, out_hbm, shares_ref, active_ref, sems):
        copies = start_all(
            [(shares_hbm.at[x], shares_ref.at[x]) for x in range(size)]
            + [(extra_hbm, active_ref.at[slots:, :])],
            sems,
        )
        total = jnp.zeros((slots, units), jnp.float32)
        for x in range(size):
            copies[x].wait()
            total += shares_ref[x].astype(jnp.float32)
        active_ref[:slots, :] = (total / (1.0 + jnp.exp(-total))).astype(jnp.bfloat16)
        copies[size].wait()
        wait_all(start_all([(active_ref, out_hbm.at[x]) for x in range(size)], sems, size + 1))

    return pl.pallas_call(
        kernel,
        out_shape=pltpu.HBM((size, slots + more, units), jnp.bfloat16),
        in_specs=[pl.BlockSpec(memory_space=pl.ANY)] * 2,
        out_specs=HBM,
        scratch_shapes=[
            pltpu.VMEM((size, slots, units), jnp.bfloat16),
            pltpu.VMEM((slots + more, units), jnp.bfloat16),
            pltpu.SemaphoreType.DMA((2 * size + 1,)),
        ],
        cost_estimate=pl.CostEstimate(
            flops=8 * slots * units,
            bytes_accessed=4 * size * slots * units,
            transcendentals=slots * units,
        ),
        compiler_params=pltpu.CompilerParams(vmem_limit_bytes=VMEM_LIMIT),
        name="expert_silu",
    )(shares, extra)


def expert_down(active, weights, experts, capacity):
    size, _, units = active.shape
    part = weights.shape[1]
    slots = experts * capacity

    def kernel(active_ref, weights_ref, out_ref):
        me = lax.axis_index("hg")
        total = jnp.zeros((slots, part), jnp.float32)
        for d in range(size):
            owner = lax.rem(me + size - d, size)
            total += jnp.dot(
                active_ref[owner, :slots, :], weights_ref[d * units:(d + 1) * units, :],
                preferred_element_type=jnp.float32,
            )
        out_ref[...] = total.astype(jnp.bfloat16).reshape(experts, capacity, part)

    return pl.pallas_call(
        kernel,
        out_shape=jax.ShapeDtypeStruct((experts, capacity, part), jnp.bfloat16),
        cost_estimate=pl.CostEstimate(
            flops=2 * slots * size * part * units,
            bytes_accessed=2 * (slots * size * units + size * part * units + slots * part),
            transcendentals=0,
        ),
        compiler_params=pltpu.CompilerParams(vmem_limit_bytes=VMEM_LIMIT),
        name="expert_down",
    )(active, weights)


def on_device(
    queries,
    latent_cache,
    lengths,
    residual,
    partials,
    norm_gain,
    router,
    expert_ids,
    up_proj,
    down_proj,
):
    size = lax.axis_size("hg")
    row_count, feature_width = residual.shape
    top_count = expert_ids.shape[1]
    experts = lax.axis_size("dp") * up_proj.shape[0]
    capacity = min(row_count, max(2, 2 * row_count * top_count // experts))
    unit_count = up_proj.shape[2]
    slots = experts * capacity

    copies = jnp.broadcast_to(partials[0][None], (size,) + partials.shape[1:])
    to_next, to_back = pack_weights(up_proj[0], down_proj[0], copies, size)
    after, before = shift(to_next, 1, size), shift(to_back, size - 1, size)
    far = 4 * (feature_width // size)
    far_low, far_high = shift(after[far:], 1, size), shift(before[far:], size - 1, size)

    normed, hidden, route, outgoing = norm_and_route(
        exchange(copies), residual, norm_gain, expert_ids.T, experts, capacity
    )
    arrived = lax.all_to_all(outgoing, "dp", split_axis=0, concat_axis=0, tiled=True)

    local_logits = jnp.dot(normed, router, preferred_element_type=jnp.float32)
    high = local_logits.astype(jnp.bfloat16)
    low = (local_logits - high.astype(jnp.float32)).astype(jnp.bfloat16)
    extra = jnp.pad(
        jnp.concatenate([high, low], axis=1), ((0, 0), (0, unit_count - 2 * high.shape[1]))
    )
    own_up, own_down = own_blocks(up_proj[0], down_proj[0], normed, size)
    up_all, down_all = join_weights(own_up, own_down, after, before, far_low, far_high)
    arrived, extra, up_all, down_all = lax.optimization_barrier((arrived, extra, up_all, down_all))

    shares = exchange(expert_up(arrived, up_all))
    active = exchange(expert_silu(shares, extra))
    reduced = expert_down(active, down_all, experts, capacity)
    reduced, latent_cache = lax.optimization_barrier((reduced, latent_cache))
    returned = lax.all_to_all(reduced, "dp", split_axis=0, concat_axis=0, tiled=True)
    attended = attention(queries, latent_cache, lengths)
    gate_matrix = gates(active[:, slots:], route, experts, capacity)
    layer_out = combine(gate_matrix, returned, hidden)
    return (attended, layer_out)


def solution(mesh):
    return jax.shard_map(
        on_device,
        mesh=mesh,
        in_specs=(
            P("dp", "hg", None),
            P("dp", "hg", None),
            P("dp"),
            P("dp", None),
            P("hg", "dp", None),
            P(),
            P(None, "hg"),
            P("dp", None),
            P("dp", None, "hg"),
            P("dp", "hg", None),
        ),
        out_specs=(P("dp", "hg", None), P("dp", "hg")),
        check_vma=False,
    )
```

```python
import jax
import jax.numpy as jnp
from jax import lax
from jax.experimental import pallas as pl
from jax.experimental.pallas import tpu as pltpu
from jax.sharding import PartitionSpec as P

LATENT = 512
SOFTMAX_SCALE = 192.0 ** (-0.5)
ROUTE_SCALE = 2.5
NORM_EPS = 1e-06
VMEM_LIMIT = 16 << 20
WHOLE_VMEM = 60 << 20
JOIN_FLOPS = 9 * 10 ** 9
DOWN_FLOPS = 4 * 10 ** 9
ORDER = (0, 1, 3, 2)


def shift(value, distance, size):
    return lax.ppermute(value, "hg", [(i, (i + distance) % size) for i in range(size)])


def spread(value, size):
    return lax.all_to_all(jnp.broadcast_to(value[None], (size,) + value.shape), "hg", 0, 0, tiled=True)


def exchange(value):
    return lax.all_to_all(value, "hg", 0, 0, tiled=True)


def attention(queries, latent_cache, lengths):
    size = lax.axis_size("hg")
    me = lax.axis_index("hg")
    width = latent_cache.shape[1]
    blocks = [latent_cache] + [shift(latent_cache, d, size) for d in range(1, size)]
    whole_cache = jnp.concatenate(blocks, axis=1)
    places = jnp.arange(size * width, dtype=jnp.int32)
    owner = (me - places // width + size) % size
    positions = owner * width + places % width
    scores = (
        jnp.einsum("rhc,rpc->rhp", queries, whole_cache, preferred_element_type=jnp.float32)
        * SOFTMAX_SCALE
    )
    in_range = positions[None, :] < lengths[:, None]
    scores = jnp.where(in_range[:, None, :], scores, -jnp.inf)
    largest = jnp.max(scores, axis=2, keepdims=True)
    weights = jnp.exp(scores - largest)
    probabilities = (weights / jnp.sum(weights, axis=2, keepdims=True)).astype(jnp.bfloat16)
    combined = jnp.einsum(
        "rhp,rpc->rhc",
        probabilities,
        whole_cache[:, :, :LATENT],
        preferred_element_type=jnp.float32,
    )
    return combined.astype(jnp.bfloat16)


HBM = pl.BlockSpec(memory_space=pltpu.HBM)
VMEM = pl.BlockSpec(memory_space=pltpu.VMEM)


def start_all(pairs, sems, first=0):
    copies = [
        pltpu.make_async_copy(source, target, sems.at[first + i])
        for i, (source, target) in enumerate(pairs)
    ]
    for copy in copies:
        copy.start()
    return copies


def wait_all(copies):
    for copy in copies:
        copy.wait()


def place(d, size, width):
    return pl.multiple_of(lax.rem(lax.axis_index("hg") + d, size) * width, 128)


def pack_weights(up_weights, down_weights, earlier, size):
    features, units = up_weights.shape
    part = features // size
    half = units // 2
    chunks = part // 128
    first = chunks // 2
    block = 2 * part
    length = 2 * block + first * units
    assert units == 256 and size == 4 and part % 128 == 0 and block == chunks * units

    def kernel(up_hbm, down_hbm, earlier_ref, next_hbm, back_hbm, up_ref, down_ref, far_ref, next_ref, back_ref, sems):
        ups = start_all(
            [(up_hbm.at[pl.ds(place(d, size, part), part), :], up_ref.at[i]) for i, d in enumerate((1, 2, 3))], sems
        )
        downs = start_all(
            [
                (down_hbm.at[:, pl.ds(place(d, size, part), first * 128)], down_ref.at[i])
                for i, d in enumerate((1, 3))
            ]
            + [(down_hbm.at[:, pl.ds(place(2, size, part), part)], far_ref)],
            sems, 3,
        )

        def put_up(i, to_ref, at):
            ups[i].wait()
            to_ref[at:at + part, :] = up_ref[i, :, :half]
            to_ref[at + part:at + block, :] = up_ref[i, :, half:]

        def put_down(i, to_ref):
            downs[i].wait()
            for k in range(first):
                at = 2 * block + k * units
                to_ref[at:at + units, :] = down_ref[i, :, k * 128:(k + 1) * 128]

        put_up(0, next_ref, 0)
        put_up(1, next_ref, block)
        put_down(0, next_ref)
        outs = start_all([(next_ref, next_hbm)], sems, 6)
        put_up(2, back_ref, 0)
        put_down(1, back_ref)
        downs[2].wait()
        for k in range(chunks):
            back_ref[block + k * units:block + (k + 1) * units, :] = far_ref[:, k * 128:(k + 1) * 128]
        outs += start_all([(back_ref, back_hbm)], sems, 7)
        wait_all(outs)

    dtype = up_weights.dtype
    return pl.pallas_call(
        kernel,
        out_shape=[pltpu.HBM((length, 128), dtype)] * 2,
        in_specs=[HBM, HBM, pl.BlockSpec(memory_space=pl.ANY)],
        out_specs=[HBM, HBM],
        scratch_shapes=[
            pltpu.VMEM((3, part, units), dtype),
            pltpu.VMEM((2, units, first * 128), dtype),
            pltpu.VMEM((units, part), dtype),
            pltpu.VMEM((length, 128), dtype),
            pltpu.VMEM((length, 128), dtype),
            pltpu.SemaphoreType.DMA((8,)),
        ],
        cost_estimate=pl.CostEstimate(
            flops=0, bytes_accessed=8 * features * units, transcendentals=0
        ),
        compiler_params=pltpu.CompilerParams(vmem_limit_bytes=WHOLE_VMEM),
        name="pack_weights",
    )(up_weights, down_weights, earlier)


def rest_blocks(down_weights, earlier, size):
    units, features = down_weights.shape
    part = features // size
    skip = part // 256 * 128
    width = part - skip

    def kernel(down_hbm, earlier_ref, next_hbm, back_hbm, ref, sems):
        fetched = start_all(
            [
                (down_hbm.at[:, pl.ds(pl.multiple_of(place(d, size, part) + skip, 128), width)], ref.at[i])
                for i, d in enumerate((1, 3))
            ],
            sems,
        )
        outs = []
        for i, out_hbm in enumerate((next_hbm, back_hbm)):
            fetched[i].wait()
            outs += start_all([(ref.at[i], out_hbm)], sems, 2 + i)
        wait_all(outs)

    return pl.pallas_call(
        kernel,
        out_shape=[pltpu.HBM((units, width), down_weights.dtype)] * 2,
        in_specs=[HBM, pl.BlockSpec(memory_space=pl.ANY)],
        out_specs=[HBM, HBM],
        scratch_shapes=[pltpu.VMEM((2, units, width), down_weights.dtype), pltpu.SemaphoreType.DMA((4,))],
        compiler_params=pltpu.CompilerParams(vmem_limit_bytes=WHOLE_VMEM),
        name="rest_blocks",
    )(down_weights, earlier)


def join_up_near(up_weights, after, before, size):
    features, units = up_weights.shape
    part = features // size
    half = units // 2

    def kernel(up_hbm, after_hbm, before_hbm, out_hbm, ref, sems):
        fetched = start_all(
            [(up_hbm.at[pl.ds(place(0, size, part), part), :], ref.at[:, :units])]
            + [
                (hbm.at[j * part:(j + 1) * part, :], ref.at[:, i * units + j * half:i * units + (j + 1) * half])
                for i, hbm in ((1, after_hbm), (2, before_hbm))
                for j in (0, 1)
            ],
            sems,
        )
        wait_all(fetched)
        wait_all(start_all([(ref, out_hbm.at[:, :3 * units])], sems, 5))

    dtype = up_weights.dtype
    return pl.pallas_call(
        kernel,
        out_shape=pltpu.HBM((part, size * units), dtype),
        in_specs=[HBM] * 3,
        out_specs=HBM,
        scratch_shapes=[pltpu.VMEM((part, 3 * units), dtype), pltpu.SemaphoreType.DMA((6,))],
        cost_estimate=pl.CostEstimate(
            flops=JOIN_FLOPS, bytes_accessed=12 * part * units, transcendentals=0
        ),
        compiler_params=pltpu.CompilerParams(vmem_limit_bytes=WHOLE_VMEM),
        name="join_up_near",
    )(up_weights, after, before)


def join_up_far(joined, far):
    part, width = joined.shape
    half = far.shape[1]

    def kernel(far_hbm, joined_hbm, out_hbm, ref, sems):
        wait_all(start_all(
            [(far_hbm.at[i * part:(i + 1) * part, :], ref.at[:, i * half:(i + 1) * half]) for i in (0, 1)], sems
        ))
        wait_all(start_all([(ref, out_hbm.at[:, width - 2 * half:])], sems, 2))

    return pl.pallas_call(
        kernel,
        out_shape=pltpu.HBM(joined.shape, joined.dtype),
        in_specs=[HBM] * 2,
        out_specs=HBM,
        scratch_shapes=[pltpu.VMEM((part, 2 * half), joined.dtype), pltpu.SemaphoreType.DMA((3,))],
        input_output_aliases={1: 0},
        compiler_params=pltpu.CompilerParams(vmem_limit_bytes=WHOLE_VMEM),
        name="join_up_far",
    )(far, joined)


def join_down(down_weights, after, before, after_rest, before_rest, far, size):
    units, features = down_weights.shape
    part = features // size
    chunks = part // 128
    first = chunks // 2
    block = 2 * part

    def kernel(
        down_hbm, after_hbm, before_hbm, after_rest_hbm, before_rest_hbm, far_hbm, out_hbm, near_ref, far_ref, ref, sems
    ):
        fetched = start_all(
            [
                (after_hbm.at[2 * block:, :], near_ref.at[0]),
                (before_hbm.at[2 * block:, :], near_ref.at[1]),
                (far_hbm, far_ref),
                (down_hbm.at[:, pl.ds(place(0, size, part), part)], ref.at[:units, :]),
                (after_rest_hbm, ref.at[units:2 * units, first * 128:]),
                (before_rest_hbm, ref.at[2 * units:3 * units, first * 128:]),
            ],
            sems,
        )
        for i in (0, 1):
            fetched[i].wait()
            for k in range(first):
                ref[(i + 1) * units:(i + 2) * units, k * 128:(k + 1) * 128] = near_ref[i, k * units:(k + 1) * units, :]
        fetched[2].wait()
        for k in range(chunks):
            ref[3 * units:, k * 128:(k + 1) * 128] = far_ref[k * units:(k + 1) * units, :]
        wait_all(fetched[3:])
        wait_all(start_all([(ref, out_hbm)], sems, 6))

    dtype = down_weights.dtype
    return pl.pallas_call(
        kernel,
        out_shape=pltpu.HBM((size * units, part), dtype),
        in_specs=[HBM] * 6,
        out_specs=HBM,
        scratch_shapes=[
            pltpu.VMEM((2, first * units, 128), dtype),
            pltpu.VMEM((block, 128), dtype),
            pltpu.VMEM((size * units, part), dtype),
            pltpu.SemaphoreType.DMA((7,)),
        ],
        cost_estimate=pl.CostEstimate(
            flops=DOWN_FLOPS, bytes_accessed=16 * part * units, transcendentals=0
        ),
        compiler_params=pltpu.CompilerParams(vmem_limit_bytes=WHOLE_VMEM),
        name="join_down",
    )(down_weights, after, before, after_rest, before_rest, far)


def norm_and_route(copies, residual, gain, choices, experts, capacity):
    size, rows, features = copies.shape
    part = features // size
    slots = experts * capacity
    top = choices.shape[0]

    def kernel(
        copies_ref, residual_hbm, gain_hbm, choices_hbm, normed_hbm, hidden_hbm, route_hbm, out_hbm,
        residual_ref, gain_ref, choices_ref, hidden_ref, normed_ref, route_ref, out_ref, sems,
    ):
        fetched = start_all(
            [(choices_hbm, choices_ref), (residual_hbm, residual_ref), (gain_hbm, gain_ref)], sems, 4
        )
        fetched[0].wait()
        expert = lax.div(lax.broadcasted_iota(jnp.int32, (slots, rows), 0), capacity)
        slot = lax.broadcasted_iota(jnp.int32, (slots, rows), 0) - expert * capacity
        hits = jnp.zeros((slots, rows), jnp.float32)
        for k in range(top):
            hits += jnp.where(choices_ref[k:k + 1, :] == expert, 1.0, 0.0)
        above = lax.broadcasted_iota(jnp.int32, (rows, rows), 0) < lax.broadcasted_iota(
            jnp.int32, (rows, rows), 1
        )
        earlier = jnp.dot(
            hits.astype(jnp.bfloat16), jnp.where(above, 1.0, 0.0).astype(jnp.bfloat16),
            preferred_element_type=jnp.float32,
        )
        route = jnp.where(earlier == slot.astype(jnp.float32), hits, 0.0).astype(jnp.bfloat16)
        route_ref[...] = route

        wait_all(fetched[1:])
        hidden = residual_ref[...].astype(jnp.float32)
        for x in range(size):
            hidden += copies_ref[x].astype(jnp.float32)
        hidden_ref[...] = hidden
        scale = lax.rsqrt(jnp.mean(hidden * hidden, axis=1, keepdims=True) + NORM_EPS)
        normed_ref[...] = (hidden * scale * gain_ref[...][None, :]).astype(jnp.bfloat16)
        mine = pl.ds(place(0, size, part), part)
        out_ref[...] = jnp.dot(
            route, normed_ref[:, mine], preferred_element_type=jnp.float32
        ).astype(jnp.bfloat16).reshape(experts, capacity, part)
        wait_all(start_all(
            [
                (out_ref, out_hbm),
                (normed_ref, normed_hbm),
                (hidden_ref.at[:, mine], hidden_hbm),
                (route_ref, route_hbm),
            ],
            sems,
        ))

    shapes = [
        ((rows, features), jnp.bfloat16),
        ((rows, part), jnp.float32),
        ((slots, rows), jnp.bfloat16),
        ((experts, capacity, part), jnp.bfloat16),
    ]
    return pl.pallas_call(
        kernel,
        out_shape=[pltpu.HBM(*shape) for shape in shapes],
        in_specs=[VMEM, HBM, HBM, HBM],
        out_specs=[HBM] * 4,
        scratch_shapes=[
            pltpu.VMEM(residual.shape, residual.dtype),
            pltpu.VMEM(gain.shape, gain.dtype),
            pltpu.VMEM(choices.shape, choices.dtype),
            pltpu.VMEM((rows, features), jnp.float32),
            pltpu.VMEM((rows, features), jnp.bfloat16),
            pltpu.VMEM((slots, rows), jnp.bfloat16),
            pltpu.VMEM((experts, capacity, part), jnp.bfloat16),
            pltpu.SemaphoreType.DMA((7,)),
        ],
        cost_estimate=pl.CostEstimate(
            flops=2 * slots * rows * part,
            bytes_accessed=2 * (size + 2) * rows * features + 2 * slots * part,
            transcendentals=0,
        ),
        compiler_params=pltpu.CompilerParams(vmem_limit_bytes=VMEM_LIMIT),
        name="norm_and_route",
    )(copies, residual, gain, choices)


def gates(logit_parts, route, experts, capacity):
    size, rows, lanes = logit_parts.shape
    slots = experts * capacity
    local = experts // size

    def kernel(parts_ref, route_ref, out_ref):
        expert = lax.div(lax.broadcasted_iota(jnp.int32, (slots, lanes), 0), capacity)
        lane = lax.broadcasted_iota(jnp.int32, (slots, lanes), 1)
        column = jnp.where(lane < local, lane, lane - local)
        logits = jnp.zeros((slots, rows), jnp.float32)
        for x in range(size):
            pick = (column + x * local == expert) & (lane < 2 * local)
            logits += lax.dot_general(
                jnp.where(pick, 1.0, 0.0).astype(jnp.bfloat16), parts_ref[x],
                (((1,), (1,)), ((), ())), preferred_element_type=jnp.float32,
            )
        affinity = route_ref[...].astype(jnp.float32) / (1.0 + jnp.exp(-logits))
        total = jnp.sum(affinity, axis=0, keepdims=True)
        out_ref[...] = (ROUTE_SCALE * affinity / total).astype(jnp.bfloat16)

    return pl.pallas_call(
        kernel,
        out_shape=jax.ShapeDtypeStruct((slots, rows), jnp.bfloat16),
        name="gates",
    )(logit_parts, route)


def combine(gate_matrix, returned, hidden):
    experts, capacity, part = returned.shape
    slots = experts * capacity

    def kernel(gates_hbm, returned_ref, hidden_hbm, out_ref, gates_ref, hidden_ref, sems):
        copies = start_all([(gates_hbm, gates_ref), (hidden_hbm, hidden_ref)], sems)
        wait_all(copies)
        routed = lax.dot_general(
            gates_ref[...], returned_ref[...].reshape(slots, part), (((0,), (0,)), ((), ())),
            preferred_element_type=jnp.float32,
        )
        out_ref[...] = (hidden_ref[...] + routed).astype(jnp.bfloat16)

    return pl.pallas_call(
        kernel,
        out_shape=jax.ShapeDtypeStruct(hidden.shape, jnp.bfloat16),
        in_specs=[HBM, VMEM, HBM],
        scratch_shapes=[
            pltpu.VMEM(gate_matrix.shape, gate_matrix.dtype),
            pltpu.VMEM(hidden.shape, hidden.dtype),
            pltpu.SemaphoreType.DMA((2,)),
        ],
        compiler_params=pltpu.CompilerParams(vmem_limit_bytes=VMEM_LIMIT),
        name="combine",
    )(gate_matrix, returned, hidden)


def expert_up(arrived, weights):
    size = lax.axis_size("hg")
    experts, capacity, part = arrived.shape
    slots = experts * capacity
    units = weights.shape[1] // size

    def kernel(rows_ref, weights_ref, out_ref):
        me = lax.axis_index("hg")
        rows = rows_ref[...].reshape(slots, part)
        for i, d in enumerate(ORDER):
            out_ref[lax.rem(me + size - d, size)] = jnp.dot(
                rows, weights_ref[:, i * units:(i + 1) * units],
                preferred_element_type=jnp.float32,
            ).astype(jnp.bfloat16)

    return pl.pallas_call(
        kernel,
        out_shape=jax.ShapeDtypeStruct((size, slots, units), jnp.bfloat16),
        cost_estimate=pl.CostEstimate(
            flops=2 * slots * size * part * units,
            bytes_accessed=2 * (slots * part + size * part * units + size * slots * units),
            transcendentals=0,
        ),
        compiler_params=pltpu.CompilerParams(vmem_limit_bytes=VMEM_LIMIT),
        name="expert_up",
    )(arrived, weights)


def expert_silu(shares, extra):
    size, slots, units = shares.shape
    more = extra.shape[0]

    def kernel(shares_hbm, extra_hbm, out_hbm, shares_ref, active_ref, sems):
        copies = start_all(
            [(shares_hbm.at[x], shares_ref.at[x]) for x in range(size)]
            + [(extra_hbm, active_ref.at[slots:, :])],
            sems,
        )
        total = jnp.zeros((slots, units), jnp.float32)
        for x in range(size):
            copies[x].wait()
            total += shares_ref[x].astype(jnp.float32)
        active_ref[:slots, :] = (total / (1.0 + jnp.exp(-total))).astype(jnp.bfloat16)
        copies[size].wait()
        wait_all(start_all([(active_ref, out_hbm.at[x]) for x in range(size)], sems, size + 1))

    return pl.pallas_call(
        kernel,
        out_shape=pltpu.HBM((size, slots + more, units), jnp.bfloat16),
        in_specs=[pl.BlockSpec(memory_space=pl.ANY)] * 2,
        out_specs=HBM,
        scratch_shapes=[
            pltpu.VMEM((size, slots, units), jnp.bfloat16),
            pltpu.VMEM((slots + more, units), jnp.bfloat16),
            pltpu.SemaphoreType.DMA((2 * size + 1,)),
        ],
        cost_estimate=pl.CostEstimate(
            flops=8 * slots * units,
            bytes_accessed=4 * size * slots * units,
            transcendentals=slots * units,
        ),
        compiler_params=pltpu.CompilerParams(vmem_limit_bytes=VMEM_LIMIT),
        name="expert_silu",
    )(shares, extra)


def expert_down(active, weights, experts, capacity):
    size, _, units = active.shape
    part = weights.shape[1]
    slots = experts * capacity

    def kernel(active_ref, weights_ref, out_ref):
        me = lax.axis_index("hg")
        total = jnp.zeros((slots, part), jnp.float32)
        for i, d in enumerate(ORDER):
            total += jnp.dot(
                active_ref[lax.rem(me + size - d, size), :slots, :],
                weights_ref[i * units:(i + 1) * units, :],
                preferred_element_type=jnp.float32,
            )
        out_ref[...] = total.astype(jnp.bfloat16).reshape(experts, capacity, part)

    return pl.pallas_call(
        kernel,
        out_shape=jax.ShapeDtypeStruct((experts, capacity, part), jnp.bfloat16),
        cost_estimate=pl.CostEstimate(
            flops=2 * slots * size * part * units,
            bytes_accessed=2 * (slots * size * units + size * part * units + slots * part),
            transcendentals=0,
        ),
        compiler_params=pltpu.CompilerParams(vmem_limit_bytes=VMEM_LIMIT),
        name="expert_down",
    )(active, weights)


def on_device(
    queries,
    latent_cache,
    lengths,
    residual,
    partials,
    norm_gain,
    router,
    expert_ids,
    up_proj,
    down_proj,
):
    size = lax.axis_size("hg")
    row_count, feature_width = residual.shape
    top_count = expert_ids.shape[1]
    experts = lax.axis_size("dp") * up_proj.shape[0]
    capacity = min(row_count, max(2, 2 * row_count * top_count // experts))
    unit_count = up_proj.shape[2]
    slots = experts * capacity

    copies = jnp.broadcast_to(partials[0][None], (size,) + partials.shape[1:])
    to_next, to_back = pack_weights(up_proj[0], down_proj[0], copies, size)
    after, before = shift(to_next, 1, size), shift(to_back, size - 1, size)
    block = 2 * (feature_width // size)
    far_up = shift(after[block:2 * block], 1, size)
    far_down = shift(before[block:2 * block], size - 1, size)
    next_rest, back_rest = rest_blocks(down_proj[0], after, size)
    after_rest, before_rest = shift(next_rest, 1, size), shift(back_rest, size - 1, size)

    normed, hidden, route, outgoing = norm_and_route(
        exchange(copies), residual, norm_gain, expert_ids.T, experts, capacity
    )
    arrived = lax.all_to_all(outgoing, "dp", split_axis=0, concat_axis=0, tiled=True)

    local_logits = jnp.dot(normed, router, preferred_element_type=jnp.float32)
    high = local_logits.astype(jnp.bfloat16)
    low = (local_logits - high.astype(jnp.float32)).astype(jnp.bfloat16)
    extra = jnp.pad(
        jnp.concatenate([high, low], axis=1), ((0, 0), (0, unit_count - 2 * high.shape[1]))
    )
    up_all = join_up_near(up_proj[0], after, before, size)
    up_all = join_up_far(up_all, far_up)
    arrived, extra, up_all = lax.optimization_barrier((arrived, extra, up_all))
    shares = exchange(expert_up(arrived, up_all))

    down_all = join_down(down_proj[0], after, before, after_rest, before_rest, far_down, size)
    shares, down_all = lax.optimization_barrier((shares, down_all))
    active = exchange(expert_silu(shares, extra))
    reduced = expert_down(active, down_all, experts, capacity)
    reduced, latent_cache = lax.optimization_barrier((reduced, latent_cache))
    returned = lax.all_to_all(reduced, "dp", split_axis=0, concat_axis=0, tiled=True)
    attended = attention(queries, latent_cache, lengths)
    gate_matrix = gates(active[:, slots:], route, experts, capacity)
    layer_out = combine(gate_matrix, returned, hidden)
    return (attended, layer_out)


def solution(mesh):
    return jax.shard_map(
        on_device,
        mesh=mesh,
        in_specs=(
            P("dp", "hg", None),
            P("dp", "hg", None),
            P("dp"),
            P("dp", None),
            P("hg", "dp", None),
            P(),
            P(None, "hg"),
            P("dp", None),
            P("dp", None, "hg"),
            P("dp", "hg", None),
        ),
        out_specs=(P("dp", "hg", None), P("dp", "hg")),
        check_vma=False,
    )
```

```python
import jax
import jax.numpy as jnp
from jax import lax
from jax.experimental import pallas as pl
from jax.experimental.pallas import tpu as pltpu
from jax.sharding import PartitionSpec as P

LATENT = 512
SOFTMAX_SCALE = 192.0 ** (-0.5)
ROUTE_SCALE = 2.5
NORM_EPS = 1e-06
VMEM_LIMIT = 16 << 20
WHOLE_VMEM = 60 << 20
JOIN_FLOPS = 9 * 10 ** 9
DOWN_FLOPS = 4 * 10 ** 9
ORDER = (0, 1, 3, 2)


def shift(value, distance, size):
    return lax.ppermute(value, "hg", [(i, (i + distance) % size) for i in range(size)])


def spread(value, size):
    return lax.all_to_all(jnp.broadcast_to(value[None], (size,) + value.shape), "hg", 0, 0, tiled=True)


def exchange(value):
    return lax.all_to_all(value, "hg", 0, 0, tiled=True)


def attention(queries, latent_cache, lengths):
    size = lax.axis_size("hg")
    me = lax.axis_index("hg")
    width = latent_cache.shape[1]
    blocks = [latent_cache] + [shift(latent_cache, d, size) for d in range(1, size)]
    whole_cache = jnp.concatenate(blocks, axis=1)
    places = jnp.arange(size * width, dtype=jnp.int32)
    owner = (me - places // width + size) % size
    positions = owner * width + places % width
    scores = (
        jnp.einsum("rhc,rpc->rhp", queries, whole_cache, preferred_element_type=jnp.float32)
        * SOFTMAX_SCALE
    )
    in_range = positions[None, :] < lengths[:, None]
    scores = jnp.where(in_range[:, None, :], scores, -jnp.inf)
    largest = jnp.max(scores, axis=2, keepdims=True)
    weights = jnp.exp(scores - largest)
    probabilities = (weights / jnp.sum(weights, axis=2, keepdims=True)).astype(jnp.bfloat16)
    combined = jnp.einsum(
        "rhp,rpc->rhc",
        probabilities,
        whole_cache[:, :, :LATENT],
        preferred_element_type=jnp.float32,
    )
    return combined.astype(jnp.bfloat16)


HBM = pl.BlockSpec(memory_space=pltpu.HBM)
VMEM = pl.BlockSpec(memory_space=pltpu.VMEM)


def start_all(pairs, sems, first=0):
    copies = [
        pltpu.make_async_copy(source, target, sems.at[first + i])
        for i, (source, target) in enumerate(pairs)
    ]
    for copy in copies:
        copy.start()
    return copies


def wait_all(copies):
    for copy in copies:
        copy.wait()


def place(d, size, width):
    return pl.multiple_of(lax.rem(lax.axis_index("hg") + d, size) * width, 128)


def pack_weights(up_weights, down_weights, earlier, size):
    features, units = up_weights.shape
    part = features // size
    half = units // 2
    chunks = part // 128
    first = chunks // 2
    block = 2 * part
    length = 2 * block + first * units
    assert units == 256 and size == 4 and part % 128 == 0 and block == chunks * units

    def kernel(up_hbm, down_hbm, earlier_ref, next_hbm, back_hbm, up_ref, down_ref, far_ref, next_ref, back_ref, sems):
        ups = start_all(
            [(up_hbm.at[pl.ds(place(d, size, part), part), :], up_ref.at[i]) for i, d in enumerate((1, 2, 3))], sems
        )
        downs = start_all(
            [
                (down_hbm.at[:, pl.ds(place(d, size, part), first * 128)], down_ref.at[i])
                for i, d in enumerate((1, 3))
            ]
            + [(down_hbm.at[:, pl.ds(place(2, size, part), part)], far_ref)],
            sems, 3,
        )

        def put_up(i, to_ref, at):
            ups[i].wait()
            to_ref[at:at + part, :] = up_ref[i, :, :half]
            to_ref[at + part:at + block, :] = up_ref[i, :, half:]

        def put_down(i, to_ref):
            downs[i].wait()
            for k in range(first):
                at = 2 * block + k * units
                to_ref[at:at + units, :] = down_ref[i, :, k * 128:(k + 1) * 128]

        put_up(0, next_ref, 0)
        put_up(1, next_ref, block)
        put_down(0, next_ref)
        outs = start_all([(next_ref, next_hbm)], sems, 6)
        put_up(2, back_ref, 0)
        put_down(1, back_ref)
        downs[2].wait()
        for k in range(chunks):
            back_ref[block + k * units:block + (k + 1) * units, :] = far_ref[:, k * 128:(k + 1) * 128]
        outs += start_all([(back_ref, back_hbm)], sems, 7)
        wait_all(outs)

    dtype = up_weights.dtype
    return pl.pallas_call(
        kernel,
        out_shape=[pltpu.HBM((length, 128), dtype)] * 2,
        in_specs=[HBM, HBM, pl.BlockSpec(memory_space=pl.ANY)],
        out_specs=[HBM, HBM],
        scratch_shapes=[
            pltpu.VMEM((3, part, units), dtype),
            pltpu.VMEM((2, units, first * 128), dtype),
            pltpu.VMEM((units, part), dtype),
            pltpu.VMEM((length, 128), dtype),
            pltpu.VMEM((length, 128), dtype),
            pltpu.SemaphoreType.DMA((8,)),
        ],
        cost_estimate=pl.CostEstimate(
            flops=0, bytes_accessed=8 * features * units, transcendentals=0
        ),
        compiler_params=pltpu.CompilerParams(vmem_limit_bytes=WHOLE_VMEM),
        name="pack_weights",
    )(up_weights, down_weights, earlier)


def rest_blocks(down_weights, earlier, size):
    units, features = down_weights.shape
    part = features // size
    skip = part // 256 * 128
    width = part - skip

    def kernel(down_hbm, earlier_ref, next_hbm, back_hbm, ref, sems):
        fetched = start_all(
            [
                (down_hbm.at[:, pl.ds(pl.multiple_of(place(d, size, part) + skip, 128), width)], ref.at[i])
                for i, d in enumerate((1, 3))
            ],
            sems,
        )
        outs = []
        for i, out_hbm in enumerate((next_hbm, back_hbm)):
            fetched[i].wait()
            outs += start_all([(ref.at[i], out_hbm)], sems, 2 + i)
        wait_all(outs)

    return pl.pallas_call(
        kernel,
        out_shape=[pltpu.HBM((units, width), down_weights.dtype)] * 2,
        in_specs=[HBM, pl.BlockSpec(memory_space=pl.ANY)],
        out_specs=[HBM, HBM],
        scratch_shapes=[pltpu.VMEM((2, units, width), down_weights.dtype), pltpu.SemaphoreType.DMA((4,))],
        compiler_params=pltpu.CompilerParams(vmem_limit_bytes=WHOLE_VMEM),
        name="rest_blocks",
    )(down_weights, earlier)


def join_up_near(up_weights, after, before, size):
    features, units = up_weights.shape
    part = features // size
    half = units // 2

    def kernel(up_hbm, after_hbm, before_hbm, out_hbm, ref, sems):
        fetched = start_all(
            [(up_hbm.at[pl.ds(place(0, size, part), part), :], ref.at[:, :units])]
            + [
                (hbm.at[j * part:(j + 1) * part, :], ref.at[:, i * units + j * half:i * units + (j + 1) * half])
                for i, hbm in ((1, after_hbm), (2, before_hbm))
                for j in (0, 1)
            ],
            sems,
        )
        wait_all(fetched)
        wait_all(start_all([(ref, out_hbm)], sems, 5))

    dtype = up_weights.dtype
    return pl.pallas_call(
        kernel,
        out_shape=pltpu.HBM((part, 3 * units), dtype),
        in_specs=[HBM] * 3,
        out_specs=HBM,
        scratch_shapes=[pltpu.VMEM((part, 3 * units), dtype), pltpu.SemaphoreType.DMA((6,))],
        cost_estimate=pl.CostEstimate(
            flops=JOIN_FLOPS, bytes_accessed=12 * part * units, transcendentals=0
        ),
        compiler_params=pltpu.CompilerParams(vmem_limit_bytes=WHOLE_VMEM),
        name="join_up_near",
    )(up_weights, after, before)


def join_up_far(joined, far):
    part, width = joined.shape
    half = far.shape[1]

    def kernel(far_ref, joined_hbm, out_ref, sems):
        fetched = start_all([(joined_hbm, out_ref.at[:, :width])], sems)
        out_ref[:, width:width + half] = far_ref[:part, :]
        out_ref[:, width + half:] = far_ref[part:, :]
        wait_all(fetched)

    return pl.pallas_call(
        kernel,
        out_shape=jax.ShapeDtypeStruct((part, width + 2 * half), joined.dtype),
        in_specs=[VMEM, HBM],
        out_specs=VMEM,
        scratch_shapes=[pltpu.SemaphoreType.DMA((1,))],
        compiler_params=pltpu.CompilerParams(vmem_limit_bytes=VMEM_LIMIT),
        name="join_up_far",
    )(far, joined)


def join_down(down_weights, after, before, after_rest, before_rest, far, size):
    units, features = down_weights.shape
    part = features // size
    chunks = part // 128
    first = chunks // 2
    block = 2 * part

    def kernel(
        down_hbm, after_hbm, before_hbm, after_rest_hbm, before_rest_hbm, far_hbm, out_hbm, near_ref, far_ref, ref, sems
    ):
        fetched = start_all(
            [
                (after_hbm.at[2 * block:, :], near_ref.at[0]),
                (before_hbm.at[2 * block:, :], near_ref.at[1]),
                (far_hbm, far_ref),
                (down_hbm.at[:, pl.ds(place(0, size, part), part)], ref.at[:units, :]),
                (after_rest_hbm, ref.at[units:2 * units, first * 128:]),
                (before_rest_hbm, ref.at[2 * units:3 * units, first * 128:]),
            ],
            sems,
        )
        for i in (0, 1):
            fetched[i].wait()
            for k in range(first):
                ref[(i + 1) * units:(i + 2) * units, k * 128:(k + 1) * 128] = near_ref[i, k * units:(k + 1) * units, :]
        fetched[2].wait()
        for k in range(chunks):
            ref[3 * units:, k * 128:(k + 1) * 128] = far_ref[k * units:(k + 1) * units, :]
        wait_all(fetched[3:])
        wait_all(start_all([(ref, out_hbm)], sems, 6))

    dtype = down_weights.dtype
    return pl.pallas_call(
        kernel,
        out_shape=pltpu.HBM((size * units, part), dtype),
        in_specs=[HBM] * 6,
        out_specs=HBM,
        scratch_shapes=[
            pltpu.VMEM((2, first * units, 128), dtype),
            pltpu.VMEM((block, 128), dtype),
            pltpu.VMEM((size * units, part), dtype),
            pltpu.SemaphoreType.DMA((7,)),
        ],
        cost_estimate=pl.CostEstimate(
            flops=DOWN_FLOPS, bytes_accessed=16 * part * units, transcendentals=0
        ),
        compiler_params=pltpu.CompilerParams(vmem_limit_bytes=WHOLE_VMEM),
        name="join_down",
    )(down_weights, after, before, after_rest, before_rest, far)


def norm_and_route(copies, residual, gain, choices, experts, capacity):
    size, rows, features = copies.shape
    part = features // size
    slots = experts * capacity
    top = choices.shape[0]

    def kernel(
        copies_ref, residual_hbm, gain_hbm, choices_hbm, normed_hbm, hidden_hbm, route_hbm, out_hbm,
        residual_ref, gain_ref, choices_ref, hidden_ref, normed_ref, route_ref, out_ref, sems,
    ):
        fetched = start_all(
            [(choices_hbm, choices_ref), (residual_hbm, residual_ref), (gain_hbm, gain_ref)], sems, 4
        )
        fetched[0].wait()
        expert = lax.div(lax.broadcasted_iota(jnp.int32, (slots, rows), 0), capacity)
        slot = lax.broadcasted_iota(jnp.int32, (slots, rows), 0) - expert * capacity
        hits = jnp.zeros((slots, rows), jnp.float32)
        for k in range(top):
            hits += jnp.where(choices_ref[k:k + 1, :] == expert, 1.0, 0.0)
        above = lax.broadcasted_iota(jnp.int32, (rows, rows), 0) < lax.broadcasted_iota(
            jnp.int32, (rows, rows), 1
        )
        earlier = jnp.dot(
            hits.astype(jnp.bfloat16), jnp.where(above, 1.0, 0.0).astype(jnp.bfloat16),
            preferred_element_type=jnp.float32,
        )
        route = jnp.where(earlier == slot.astype(jnp.float32), hits, 0.0).astype(jnp.bfloat16)
        route_ref[...] = route

        wait_all(fetched[1:])
        hidden = residual_ref[...].astype(jnp.float32)
        for x in range(size):
            hidden += copies_ref[x].astype(jnp.float32)
        hidden_ref[...] = hidden
        scale = lax.rsqrt(jnp.mean(hidden * hidden, axis=1, keepdims=True) + NORM_EPS)
        normed_ref[...] = (hidden * scale * gain_ref[...][None, :]).astype(jnp.bfloat16)
        mine = pl.ds(place(0, size, part), part)
        out_ref[...] = jnp.dot(
            route, normed_ref[:, mine], preferred_element_type=jnp.float32
        ).astype(jnp.bfloat16).reshape(experts, capacity, part)
        wait_all(start_all(
            [
                (out_ref, out_hbm),
                (normed_ref, normed_hbm),
                (hidden_ref.at[:, mine], hidden_hbm),
                (route_ref, route_hbm),
            ],
            sems,
        ))

    shapes = [
        ((rows, features), jnp.bfloat16),
        ((rows, part), jnp.float32),
        ((slots, rows), jnp.bfloat16),
        ((experts, capacity, part), jnp.bfloat16),
    ]
    return pl.pallas_call(
        kernel,
        out_shape=[pltpu.HBM(*shape) for shape in shapes],
        in_specs=[VMEM, HBM, HBM, HBM],
        out_specs=[HBM] * 4,
        scratch_shapes=[
            pltpu.VMEM(residual.shape, residual.dtype),
            pltpu.VMEM(gain.shape, gain.dtype),
            pltpu.VMEM(choices.shape, choices.dtype),
            pltpu.VMEM((rows, features), jnp.float32),
            pltpu.VMEM((rows, features), jnp.bfloat16),
            pltpu.VMEM((slots, rows), jnp.bfloat16),
            pltpu.VMEM((experts, capacity, part), jnp.bfloat16),
            pltpu.SemaphoreType.DMA((7,)),
        ],
        cost_estimate=pl.CostEstimate(
            flops=2 * slots * rows * part,
            bytes_accessed=2 * (size + 2) * rows * features + 2 * slots * part,
            transcendentals=0,
        ),
        compiler_params=pltpu.CompilerParams(vmem_limit_bytes=VMEM_LIMIT),
        name="norm_and_route",
    )(copies, residual, gain, choices)


def gates(logit_parts, route, experts, capacity):
    size, rows, lanes = logit_parts.shape
    slots = experts * capacity
    local = experts // size

    def kernel(parts_ref, route_ref, out_ref):
        expert = lax.div(lax.broadcasted_iota(jnp.int32, (slots, lanes), 0), capacity)
        lane = lax.broadcasted_iota(jnp.int32, (slots, lanes), 1)
        column = jnp.where(lane < local, lane, lane - local)
        logits = jnp.zeros((slots, rows), jnp.float32)
        for x in range(size):
            pick = (column + x * local == expert) & (lane < 2 * local)
            logits += lax.dot_general(
                jnp.where(pick, 1.0, 0.0).astype(jnp.bfloat16), parts_ref[x],
                (((1,), (1,)), ((), ())), preferred_element_type=jnp.float32,
            )
        affinity = route_ref[...].astype(jnp.float32) / (1.0 + jnp.exp(-logits))
        total = jnp.sum(affinity, axis=0, keepdims=True)
        out_ref[...] = (ROUTE_SCALE * affinity / total).astype(jnp.bfloat16)

    return pl.pallas_call(
        kernel,
        out_shape=jax.ShapeDtypeStruct((slots, rows), jnp.bfloat16),
        name="gates",
    )(logit_parts, route)


def combine(gate_matrix, returned, hidden):
    experts, capacity, part = returned.shape
    slots = experts * capacity

    def kernel(gates_hbm, returned_ref, hidden_hbm, out_ref, gates_ref, hidden_ref, sems):
        copies = start_all([(gates_hbm, gates_ref), (hidden_hbm, hidden_ref)], sems)
        wait_all(copies)
        routed = lax.dot_general(
            gates_ref[...], returned_ref[...].reshape(slots, part), (((0,), (0,)), ((), ())),
            preferred_element_type=jnp.float32,
        )
        out_ref[...] = (hidden_ref[...] + routed).astype(jnp.bfloat16)

    return pl.pallas_call(
        kernel,
        out_shape=jax.ShapeDtypeStruct(hidden.shape, jnp.bfloat16),
        in_specs=[HBM, VMEM, HBM],
        scratch_shapes=[
            pltpu.VMEM(gate_matrix.shape, gate_matrix.dtype),
            pltpu.VMEM(hidden.shape, hidden.dtype),
            pltpu.SemaphoreType.DMA((2,)),
        ],
        compiler_params=pltpu.CompilerParams(vmem_limit_bytes=VMEM_LIMIT),
        name="combine",
    )(gate_matrix, returned, hidden)


def expert_up(arrived, weights):
    size = lax.axis_size("hg")
    experts, capacity, part = arrived.shape
    slots = experts * capacity
    units = weights.shape[1] // size

    def kernel(rows_ref, weights_ref, out_ref):
        me = lax.axis_index("hg")
        rows = rows_ref[...].reshape(slots, part)
        for i, d in enumerate(ORDER):
            out_ref[lax.rem(me + size - d, size)] = jnp.dot(
                rows, weights_ref[:, i * units:(i + 1) * units],
                preferred_element_type=jnp.float32,
            ).astype(jnp.bfloat16)

    return pl.pallas_call(
        kernel,
        out_shape=jax.ShapeDtypeStruct((size, slots, units), jnp.bfloat16),
        cost_estimate=pl.CostEstimate(
            flops=2 * slots * size * part * units,
            bytes_accessed=2 * (slots * part + size * part * units + size * slots * units),
            transcendentals=0,
        ),
        compiler_params=pltpu.CompilerParams(vmem_limit_bytes=VMEM_LIMIT),
        name="expert_up",
    )(arrived, weights)


def expert_silu(shares, extra):
    size, slots, units = shares.shape
    more = extra.shape[0]

    def kernel(shares_ref, extra_hbm, out_hbm, active_ref, sems):
        copies = start_all([(extra_hbm, active_ref.at[slots:, :])], sems)
        total = shares_ref[0].astype(jnp.float32)
        for x in range(1, size):
            total += shares_ref[x].astype(jnp.float32)
        active_ref[:slots, :] = (total / (1.0 + jnp.exp(-total))).astype(jnp.bfloat16)
        wait_all(copies)
        wait_all(start_all([(active_ref, out_hbm.at[x]) for x in range(size)], sems, 1))

    return pl.pallas_call(
        kernel,
        out_shape=pltpu.HBM((size, slots + more, units), jnp.bfloat16),
        in_specs=[VMEM, pl.BlockSpec(memory_space=pl.ANY)],
        out_specs=HBM,
        scratch_shapes=[
            pltpu.VMEM((slots + more, units), jnp.bfloat16),
            pltpu.SemaphoreType.DMA((size + 1,)),
        ],
        cost_estimate=pl.CostEstimate(
            flops=8 * slots * units,
            bytes_accessed=4 * size * slots * units,
            transcendentals=slots * units,
        ),
        compiler_params=pltpu.CompilerParams(vmem_limit_bytes=VMEM_LIMIT),
        name="expert_silu",
    )(shares, extra)


def expert_down(active, weights, experts, capacity):
    size, _, units = active.shape
    part = weights.shape[1]
    slots = experts * capacity

    def kernel(active_ref, weights_ref, out_ref):
        me = lax.axis_index("hg")
        total = jnp.zeros((slots, part), jnp.float32)
        for i, d in enumerate(ORDER):
            total += jnp.dot(
                active_ref[lax.rem(me + size - d, size), :slots, :],
                weights_ref[i * units:(i + 1) * units, :],
                preferred_element_type=jnp.float32,
            )
        out_ref[...] = total.astype(jnp.bfloat16).reshape(experts, capacity, part)

    return pl.pallas_call(
        kernel,
        out_shape=jax.ShapeDtypeStruct((experts, capacity, part), jnp.bfloat16),
        cost_estimate=pl.CostEstimate(
            flops=2 * slots * size * part * units,
            bytes_accessed=2 * (slots * size * units + size * part * units + slots * part),
            transcendentals=0,
        ),
        compiler_params=pltpu.CompilerParams(vmem_limit_bytes=VMEM_LIMIT),
        name="expert_down",
    )(active, weights)


def on_device(
    queries,
    latent_cache,
    lengths,
    residual,
    partials,
    norm_gain,
    router,
    expert_ids,
    up_proj,
    down_proj,
):
    size = lax.axis_size("hg")
    row_count, feature_width = residual.shape
    top_count = expert_ids.shape[1]
    experts = lax.axis_size("dp") * up_proj.shape[0]
    capacity = min(row_count, max(2, 2 * row_count * top_count // experts))
    unit_count = up_proj.shape[2]
    slots = experts * capacity

    copies = jnp.broadcast_to(partials[0][None], (size,) + partials.shape[1:])
    to_next, to_back = pack_weights(up_proj[0], down_proj[0], copies, size)
    after, before = shift(to_next, 1, size), shift(to_back, size - 1, size)
    block = 2 * (feature_width // size)
    far_up = shift(after[block:2 * block], 1, size)
    far_down = shift(before[block:2 * block], size - 1, size)
    normed, hidden, route, outgoing = norm_and_route(
        exchange(copies), residual, norm_gain, expert_ids.T, experts, capacity
    )
    next_rest, back_rest = rest_blocks(down_proj[0], normed, size)
    next_rest, back_rest, before = lax.optimization_barrier((next_rest, back_rest, before))
    after_rest, before_rest = shift(next_rest, 1, size), shift(back_rest, size - 1, size)
    arrived = lax.all_to_all(outgoing, "dp", split_axis=0, concat_axis=0, tiled=True)

    local_logits = jnp.dot(normed, router, preferred_element_type=jnp.float32)
    high = local_logits.astype(jnp.bfloat16)
    low = (local_logits - high.astype(jnp.float32)).astype(jnp.bfloat16)
    extra = jnp.pad(
        jnp.concatenate([high, low], axis=1), ((0, 0), (0, unit_count - 2 * high.shape[1]))
    )
    up_all = join_up_near(up_proj[0], after, before, size)
    up_all = join_up_far(up_all, far_up)
    arrived, up_all = lax.optimization_barrier((arrived, up_all))
    shares = exchange(expert_up(arrived, up_all))

    down_all = join_down(down_proj[0], after, before, after_rest, before_rest, far_down, size)
    shares, down_all = lax.optimization_barrier((shares, down_all))
    active = exchange(expert_silu(shares, extra))
    reduced = expert_down(active, down_all, experts, capacity)
    reduced, latent_cache = lax.optimization_barrier((reduced, latent_cache))
    returned = lax.all_to_all(reduced, "dp", split_axis=0, concat_axis=0, tiled=True)
    attended = attention(queries, latent_cache, lengths)
    gate_matrix = gates(active[:, slots:], route, experts, capacity)
    layer_out = combine(gate_matrix, returned, hidden)
    return (attended, layer_out)


def solution(mesh):
    return jax.shard_map(
        on_device,
        mesh=mesh,
        in_specs=(
            P("dp", "hg", None),
            P("dp", "hg", None),
            P("dp"),
            P("dp", None),
            P("hg", "dp", None),
            P(),
            P(None, "hg"),
            P("dp", None),
            P("dp", None, "hg"),
            P("dp", "hg", None),
        ),
        out_specs=(P("dp", "hg", None), P("dp", "hg")),
        check_vma=False,
    )
```

```python
import jax
import jax.numpy as jnp
from jax import lax
from jax.experimental import pallas as pl
from jax.experimental.pallas import tpu as pltpu
from jax.sharding import PartitionSpec as P

LATENT = 512
SOFTMAX_SCALE = 192.0 ** (-0.5)
ROUTE_SCALE = 2.5
NORM_EPS = 1e-06
VMEM_LIMIT = 16 << 20
WHOLE_VMEM = 60 << 20
JOIN_FLOPS = 9 * 10 ** 9
DOWN_FLOPS = 4 * 10 ** 9
ORDER = (0, 1, 3, 2)


def shift(value, distance, size):
    return lax.ppermute(value, "hg", [(i, (i + distance) % size) for i in range(size)])


def spread(value, size):
    return lax.all_to_all(jnp.broadcast_to(value[None], (size,) + value.shape), "hg", 0, 0, tiled=True)


def exchange(value):
    return lax.all_to_all(value, "hg", 0, 0, tiled=True)


def attention(queries, latent_cache, lengths):
    size = lax.axis_size("hg")
    me = lax.axis_index("hg")
    width = latent_cache.shape[1]
    blocks = [latent_cache] + [shift(latent_cache, d, size) for d in range(1, size)]
    whole_cache = jnp.concatenate(blocks, axis=1)
    places = jnp.arange(size * width, dtype=jnp.int32)
    owner = (me - places // width + size) % size
    positions = owner * width + places % width
    scores = (
        jnp.einsum("rhc,rpc->rhp", queries, whole_cache, preferred_element_type=jnp.float32)
        * SOFTMAX_SCALE
    )
    in_range = positions[None, :] < lengths[:, None]
    scores = jnp.where(in_range[:, None, :], scores, -jnp.inf)
    largest = jnp.max(scores, axis=2, keepdims=True)
    weights = jnp.exp(scores - largest)
    probabilities = (weights / jnp.sum(weights, axis=2, keepdims=True)).astype(jnp.bfloat16)
    combined = jnp.einsum(
        "rhp,rpc->rhc",
        probabilities,
        whole_cache[:, :, :LATENT],
        preferred_element_type=jnp.float32,
    )
    return combined.astype(jnp.bfloat16)


HBM = pl.BlockSpec(memory_space=pltpu.HBM)
VMEM = pl.BlockSpec(memory_space=pltpu.VMEM)


def start_all(pairs, sems, first=0):
    copies = [
        pltpu.make_async_copy(source, target, sems.at[first + i])
        for i, (source, target) in enumerate(pairs)
    ]
    for copy in copies:
        copy.start()
    return copies


def wait_all(copies):
    for copy in copies:
        copy.wait()


def place(d, size, width):
    return pl.multiple_of(lax.rem(lax.axis_index("hg") + d, size) * width, 128)


def pack_weights(up_weights, down_weights, earlier, size):
    features, units = up_weights.shape
    part = features // size
    half = units // 2
    chunks = part // 128
    first = chunks // 2
    block = 2 * part
    length = 2 * block + first * units
    assert units == 256 and size == 4 and part % 128 == 0 and block == chunks * units

    def kernel(up_hbm, down_hbm, earlier_ref, next_hbm, back_hbm, up_ref, down_ref, far_ref, next_ref, back_ref, sems):
        ups = start_all(
            [(up_hbm.at[pl.ds(place(d, size, part), part), :], up_ref.at[i]) for i, d in enumerate((1, 2, 3))], sems
        )
        downs = start_all(
            [
                (down_hbm.at[:, pl.ds(place(d, size, part), first * 128)], down_ref.at[i])
                for i, d in enumerate((1, 3))
            ]
            + [(down_hbm.at[:, pl.ds(place(2, size, part), part)], far_ref)],
            sems, 3,
        )

        def put_up(i, to_ref, at):
            ups[i].wait()
            to_ref[at:at + part, :] = up_ref[i, :, :half]
            to_ref[at + part:at + block, :] = up_ref[i, :, half:]

        def put_down(i, to_ref):
            downs[i].wait()
            for k in range(first):
                at = 2 * block + k * units
                to_ref[at:at + units, :] = down_ref[i, :, k * 128:(k + 1) * 128]

        put_up(0, next_ref, 0)
        put_up(1, next_ref, block)
        put_down(0, next_ref)
        outs = start_all([(next_ref, next_hbm)], sems, 6)
        put_up(2, back_ref, 0)
        put_down(1, back_ref)
        downs[2].wait()
        for k in range(chunks):
            back_ref[block + k * units:block + (k + 1) * units, :] = far_ref[:, k * 128:(k + 1) * 128]
        outs += start_all([(back_ref, back_hbm)], sems, 7)
        wait_all(outs)

    dtype = up_weights.dtype
    return pl.pallas_call(
        kernel,
        out_shape=[pltpu.HBM((length, 128), dtype)] * 2,
        in_specs=[HBM, HBM, pl.BlockSpec(memory_space=pl.ANY)],
        out_specs=[HBM, HBM],
        scratch_shapes=[
            pltpu.VMEM((3, part, units), dtype),
            pltpu.VMEM((2, units, first * 128), dtype),
            pltpu.VMEM((units, part), dtype),
            pltpu.VMEM((length, 128), dtype),
            pltpu.VMEM((length, 128), dtype),
            pltpu.SemaphoreType.DMA((8,)),
        ],
        cost_estimate=pl.CostEstimate(
            flops=0, bytes_accessed=8 * features * units, transcendentals=0
        ),
        compiler_params=pltpu.CompilerParams(vmem_limit_bytes=WHOLE_VMEM),
        name="pack_weights",
    )(up_weights, down_weights, earlier)


def rest_blocks(down_weights, earlier, size):
    units, features = down_weights.shape
    part = features // size
    skip = part // 256 * 128
    width = part - skip

    def kernel(down_hbm, earlier_ref, next_hbm, back_hbm, ref, sems):
        fetched = start_all(
            [
                (down_hbm.at[:, pl.ds(pl.multiple_of(place(d, size, part) + skip, 128), width)], ref.at[i])
                for i, d in enumerate((1, 3))
            ],
            sems,
        )
        outs = []
        for i, out_hbm in enumerate((next_hbm, back_hbm)):
            fetched[i].wait()
            outs += start_all([(ref.at[i], out_hbm)], sems, 2 + i)
        wait_all(outs)

    return pl.pallas_call(
        kernel,
        out_shape=[pltpu.HBM((units, width), down_weights.dtype)] * 2,
        in_specs=[HBM, pl.BlockSpec(memory_space=pl.ANY)],
        out_specs=[HBM, HBM],
        scratch_shapes=[pltpu.VMEM((2, units, width), down_weights.dtype), pltpu.SemaphoreType.DMA((4,))],
        compiler_params=pltpu.CompilerParams(vmem_limit_bytes=WHOLE_VMEM),
        name="rest_blocks",
    )(down_weights, earlier)


def join_up_near(up_weights, after, before, size):
    features, units = up_weights.shape
    part = features // size
    half = units // 2

    def kernel(up_hbm, after_hbm, before_hbm, out_hbm, ref, sems):
        fetched = start_all(
            [(up_hbm.at[pl.ds(place(0, size, part), part), :], ref.at[:, :units])]
            + [
                (hbm.at[j * part:(j + 1) * part, :], ref.at[:, i * units + j * half:i * units + (j + 1) * half])
                for i, hbm in ((1, after_hbm), (2, before_hbm))
                for j in (0, 1)
            ],
            sems,
        )
        wait_all(fetched)
        wait_all(start_all([(ref, out_hbm)], sems, 5))

    dtype = up_weights.dtype
    return pl.pallas_call(
        kernel,
        out_shape=pltpu.HBM((part, 3 * units), dtype),
        in_specs=[HBM] * 3,
        out_specs=HBM,
        scratch_shapes=[pltpu.VMEM((part, 3 * units), dtype), pltpu.SemaphoreType.DMA((6,))],
        cost_estimate=pl.CostEstimate(
            flops=JOIN_FLOPS, bytes_accessed=12 * part * units, transcendentals=0
        ),
        compiler_params=pltpu.CompilerParams(vmem_limit_bytes=WHOLE_VMEM),
        name="join_up_near",
    )(up_weights, after, before)


def join_up_far(joined, far):
    part, width = joined.shape
    half = far.shape[1]

    def kernel(far_ref, joined_hbm, out_ref, sems):
        fetched = start_all([(joined_hbm, out_ref.at[:, :width])], sems)
        out_ref[:, width:width + half] = far_ref[:part, :]
        out_ref[:, width + half:] = far_ref[part:, :]
        wait_all(fetched)

    return pl.pallas_call(
        kernel,
        out_shape=jax.ShapeDtypeStruct((part, width + 2 * half), joined.dtype),
        in_specs=[VMEM, HBM],
        out_specs=VMEM,
        scratch_shapes=[pltpu.SemaphoreType.DMA((1,))],
        compiler_params=pltpu.CompilerParams(vmem_limit_bytes=VMEM_LIMIT),
        name="join_up_far",
    )(far, joined)


def join_down(down_weights, after, before, after_rest, before_rest, far, size):
    units, features = down_weights.shape
    part = features // size
    chunks = part // 128
    first = chunks // 2
    block = 2 * part

    def kernel(
        down_hbm, after_hbm, before_hbm, after_rest_hbm, before_rest_hbm, far_hbm, out_hbm, near_ref, far_ref, ref, sems
    ):
        fetched = start_all(
            [
                (after_hbm.at[2 * block:, :], near_ref.at[0]),
                (before_hbm.at[2 * block:, :], near_ref.at[1]),
                (far_hbm, far_ref),
                (down_hbm.at[:, pl.ds(place(0, size, part), part)], ref.at[:units, :]),
                (after_rest_hbm, ref.at[units:2 * units, first * 128:]),
                (before_rest_hbm, ref.at[2 * units:3 * units, first * 128:]),
            ],
            sems,
        )
        for i in (0, 1):
            fetched[i].wait()
            for k in range(first):
                ref[(i + 1) * units:(i + 2) * units, k * 128:(k + 1) * 128] = near_ref[i, k * units:(k + 1) * units, :]
        fetched[2].wait()
        for k in range(chunks):
            ref[3 * units:, k * 128:(k + 1) * 128] = far_ref[k * units:(k + 1) * units, :]
        wait_all(fetched[3:])
        wait_all(start_all([(ref, out_hbm)], sems, 6))

    dtype = down_weights.dtype
    return pl.pallas_call(
        kernel,
        out_shape=pltpu.HBM((size * units, part), dtype),
        in_specs=[HBM] * 6,
        out_specs=HBM,
        scratch_shapes=[
            pltpu.VMEM((2, first * units, 128), dtype),
            pltpu.VMEM((block, 128), dtype),
            pltpu.VMEM((size * units, part), dtype),
            pltpu.SemaphoreType.DMA((7,)),
        ],
        cost_estimate=pl.CostEstimate(
            flops=DOWN_FLOPS, bytes_accessed=16 * part * units, transcendentals=0
        ),
        compiler_params=pltpu.CompilerParams(vmem_limit_bytes=WHOLE_VMEM),
        name="join_down",
    )(down_weights, after, before, after_rest, before_rest, far)


def norm_and_route(copies, residual, gain, choices, experts, capacity):
    size, rows, features = copies.shape
    part = features // size
    slots = experts * capacity
    top = choices.shape[0]

    def kernel(
        copies_ref, residual_ref, gain_ref, choices_ref, normed_hbm, hidden_hbm, route_hbm, out_hbm,
        hidden_ref, normed_ref, route_ref, out_ref, sems,
    ):
        expert = lax.div(lax.broadcasted_iota(jnp.int32, (slots, rows), 0), capacity)
        slot = lax.broadcasted_iota(jnp.int32, (slots, rows), 0) - expert * capacity
        hits = jnp.zeros((slots, rows), jnp.float32)
        for k in range(top):
            hits += jnp.where(choices_ref[k:k + 1, :] == expert, 1.0, 0.0)
        above = lax.broadcasted_iota(jnp.int32, (rows, rows), 0) < lax.broadcasted_iota(
            jnp.int32, (rows, rows), 1
        )
        earlier = jnp.dot(
            hits.astype(jnp.bfloat16), jnp.where(above, 1.0, 0.0).astype(jnp.bfloat16),
            preferred_element_type=jnp.float32,
        )
        route = jnp.where(earlier == slot.astype(jnp.float32), hits, 0.0).astype(jnp.bfloat16)
        route_ref[...] = route

        hidden = residual_ref[...].astype(jnp.float32)
        for x in range(size):
            hidden += copies_ref[x].astype(jnp.float32)
        hidden_ref[...] = hidden
        scale = lax.rsqrt(jnp.mean(hidden * hidden, axis=1, keepdims=True) + NORM_EPS)
        normed_ref[...] = (hidden * scale * gain_ref[...][None, :]).astype(jnp.bfloat16)
        mine = pl.ds(place(0, size, part), part)
        outs = start_all(
            [(normed_ref, normed_hbm), (hidden_ref.at[:, mine], hidden_hbm), (route_ref, route_hbm)], sems
        )
        out_ref[...] = jnp.dot(
            route, normed_ref[:, mine], preferred_element_type=jnp.float32
        ).astype(jnp.bfloat16).reshape(experts, capacity, part)
        wait_all(outs + start_all([(out_ref, out_hbm)], sems, 3))

    shapes = [
        ((rows, features), jnp.bfloat16),
        ((rows, part), jnp.float32),
        ((slots, rows), jnp.bfloat16),
        ((experts, capacity, part), jnp.bfloat16),
    ]
    return pl.pallas_call(
        kernel,
        out_shape=[pltpu.HBM(*shape) for shape in shapes],
        out_specs=[HBM] * 4,
        scratch_shapes=[
            pltpu.VMEM((rows, features), jnp.float32),
            pltpu.VMEM((rows, features), jnp.bfloat16),
            pltpu.VMEM((slots, rows), jnp.bfloat16),
            pltpu.VMEM((experts, capacity, part), jnp.bfloat16),
            pltpu.SemaphoreType.DMA((4,)),
        ],
        cost_estimate=pl.CostEstimate(
            flops=2 * slots * rows * part,
            bytes_accessed=2 * (size + 2) * rows * features + 2 * slots * part,
            transcendentals=0,
        ),
        compiler_params=pltpu.CompilerParams(vmem_limit_bytes=VMEM_LIMIT),
        name="norm_and_route",
    )(copies, residual, gain, choices)


def gates(logit_parts, route, experts, capacity):
    size, rows, lanes = logit_parts.shape
    slots = experts * capacity
    local = experts // size

    def kernel(parts_ref, route_ref, out_ref):
        expert = lax.div(lax.broadcasted_iota(jnp.int32, (slots, lanes), 0), capacity)
        lane = lax.broadcasted_iota(jnp.int32, (slots, lanes), 1)
        column = jnp.where(lane < local, lane, lane - local)
        logits = jnp.zeros((slots, rows), jnp.float32)
        for x in range(size):
            pick = (column + x * local == expert) & (lane < 2 * local)
            logits += lax.dot_general(
                jnp.where(pick, 1.0, 0.0).astype(jnp.bfloat16), parts_ref[x],
                (((1,), (1,)), ((), ())), preferred_element_type=jnp.float32,
            )
        affinity = route_ref[...].astype(jnp.float32) / (1.0 + jnp.exp(-logits))
        total = jnp.sum(affinity, axis=0, keepdims=True)
        out_ref[...] = (ROUTE_SCALE * affinity / total).astype(jnp.bfloat16)

    return pl.pallas_call(
        kernel,
        out_shape=jax.ShapeDtypeStruct((slots, rows), jnp.bfloat16),
        name="gates",
    )(logit_parts, route)


def combine(gate_matrix, returned, hidden):
    experts, capacity, part = returned.shape
    slots = experts * capacity

    def kernel(gates_hbm, returned_ref, hidden_hbm, out_ref, gates_ref, hidden_ref, sems):
        copies = start_all([(gates_hbm, gates_ref), (hidden_hbm, hidden_ref)], sems)
        wait_all(copies)
        routed = lax.dot_general(
            gates_ref[...], returned_ref[...].reshape(slots, part), (((0,), (0,)), ((), ())),
            preferred_element_type=jnp.float32,
        )
        out_ref[...] = (hidden_ref[...] + routed).astype(jnp.bfloat16)

    return pl.pallas_call(
        kernel,
        out_shape=jax.ShapeDtypeStruct(hidden.shape, jnp.bfloat16),
        in_specs=[HBM, VMEM, HBM],
        scratch_shapes=[
            pltpu.VMEM(gate_matrix.shape, gate_matrix.dtype),
            pltpu.VMEM(hidden.shape, hidden.dtype),
            pltpu.SemaphoreType.DMA((2,)),
        ],
        compiler_params=pltpu.CompilerParams(vmem_limit_bytes=VMEM_LIMIT),
        name="combine",
    )(gate_matrix, returned, hidden)


def expert_up(arrived, weights):
    size = lax.axis_size("hg")
    experts, capacity, part = arrived.shape
    slots = experts * capacity
    units = weights.shape[1] // size

    def kernel(rows_ref, weights_ref, out_hbm, out_ref, sems):
        me = lax.axis_index("hg")
        rows = rows_ref[...].reshape(slots, part)
        outs = []
        for i, d in enumerate(ORDER):
            out_ref[i] = jnp.dot(
                rows, weights_ref[:, i * units:(i + 1) * units],
                preferred_element_type=jnp.float32,
            ).astype(jnp.bfloat16)
            outs += start_all([(out_ref.at[i], out_hbm.at[lax.rem(me + size - d, size)])], sems, i)
        wait_all(outs)

    return pl.pallas_call(
        kernel,
        out_shape=pltpu.HBM((size, slots, units), jnp.bfloat16),
        in_specs=[VMEM, VMEM],
        out_specs=HBM,
        scratch_shapes=[
            pltpu.VMEM((size, slots, units), jnp.bfloat16), pltpu.SemaphoreType.DMA((size,))
        ],
        cost_estimate=pl.CostEstimate(
            flops=2 * slots * size * part * units,
            bytes_accessed=2 * (slots * part + size * part * units + size * slots * units),
            transcendentals=0,
        ),
        compiler_params=pltpu.CompilerParams(vmem_limit_bytes=VMEM_LIMIT),
        name="expert_up",
    )(arrived, weights)


def expert_silu(shares, extra):
    size, slots, units = shares.shape
    more = extra.shape[0]

    def kernel(shares_ref, extra_hbm, out_hbm, active_ref, sems):
        copies = start_all([(extra_hbm, active_ref.at[slots:, :])], sems)
        total = shares_ref[0].astype(jnp.float32)
        for x in range(1, size):
            total += shares_ref[x].astype(jnp.float32)
        active_ref[:slots, :] = (total / (1.0 + jnp.exp(-total))).astype(jnp.bfloat16)
        wait_all(copies)
        wait_all(start_all([(active_ref, out_hbm.at[x]) for x in range(size)], sems, 1))

    return pl.pallas_call(
        kernel,
        out_shape=pltpu.HBM((size, slots + more, units), jnp.bfloat16),
        in_specs=[VMEM, pl.BlockSpec(memory_space=pl.ANY)],
        out_specs=HBM,
        scratch_shapes=[
            pltpu.VMEM((slots + more, units), jnp.bfloat16),
            pltpu.SemaphoreType.DMA((size + 1,)),
        ],
        cost_estimate=pl.CostEstimate(
            flops=8 * slots * units,
            bytes_accessed=4 * size * slots * units,
            transcendentals=slots * units,
        ),
        compiler_params=pltpu.CompilerParams(vmem_limit_bytes=VMEM_LIMIT),
        name="expert_silu",
    )(shares, extra)


def expert_down(active, weights, experts, capacity):
    size, _, units = active.shape
    part = weights.shape[1]
    slots = experts * capacity

    cut = experts // 2

    def kernel(active_ref, weights_ref, out_hbm, out_ref, sems):
        me = lax.axis_index("hg")
        outs = []
        for half in (0, 1):
            rows = slice(half * cut * capacity, (half + 1) * cut * capacity)
            total = jnp.zeros((cut * capacity, part), jnp.float32)
            for i, d in enumerate(ORDER):
                total += jnp.dot(
                    active_ref[lax.rem(me + size - d, size), rows, :],
                    weights_ref[i * units:(i + 1) * units, :],
                    preferred_element_type=jnp.float32,
                )
            some = slice(half * cut, (half + 1) * cut)
            out_ref[some] = total.astype(jnp.bfloat16).reshape(cut, capacity, part)
            outs += start_all([(out_ref.at[some], out_hbm.at[some])], sems, half)
        wait_all(outs)

    return pl.pallas_call(
        kernel,
        out_shape=pltpu.HBM((experts, capacity, part), jnp.bfloat16),
        in_specs=[VMEM, VMEM],
        out_specs=HBM,
        scratch_shapes=[
            pltpu.VMEM((experts, capacity, part), jnp.bfloat16), pltpu.SemaphoreType.DMA((2,))
        ],
        cost_estimate=pl.CostEstimate(
            flops=2 * slots * size * part * units,
            bytes_accessed=2 * (slots * size * units + size * part * units + slots * part),
            transcendentals=0,
        ),
        compiler_params=pltpu.CompilerParams(vmem_limit_bytes=VMEM_LIMIT),
        name="expert_down",
    )(active, weights)


def on_device(
    queries,
    latent_cache,
    lengths,
    residual,
    partials,
    norm_gain,
    router,
    expert_ids,
    up_proj,
    down_proj,
):
    size = lax.axis_size("hg")
    row_count, feature_width = residual.shape
    top_count = expert_ids.shape[1]
    experts = lax.axis_size("dp") * up_proj.shape[0]
    capacity = min(row_count, max(2, 2 * row_count * top_count // experts))
    unit_count = up_proj.shape[2]
    slots = experts * capacity

    copies = jnp.broadcast_to(partials[0][None], (size,) + partials.shape[1:])
    to_next, to_back = pack_weights(up_proj[0], down_proj[0], copies, size)
    after, before = shift(to_next, 1, size), shift(to_back, size - 1, size)
    block = 2 * (feature_width // size)
    far_up = shift(after[block:2 * block], 1, size)
    far_down = shift(before[block:2 * block], size - 1, size)
    normed, hidden, route, outgoing = norm_and_route(
        exchange(copies), residual, norm_gain, expert_ids.T, experts, capacity
    )
    next_rest, back_rest = rest_blocks(down_proj[0], normed, size)
    next_rest, back_rest, before = lax.optimization_barrier((next_rest, back_rest, before))
    after_rest, before_rest = shift(next_rest, 1, size), shift(back_rest, size - 1, size)
    arrived = lax.all_to_all(outgoing, "dp", split_axis=0, concat_axis=0, tiled=True)

    local_logits = jnp.dot(normed, router, preferred_element_type=jnp.float32)
    high = local_logits.astype(jnp.bfloat16)
    low = (local_logits - high.astype(jnp.float32)).astype(jnp.bfloat16)
    extra = jnp.pad(
        jnp.concatenate([high, low], axis=1), ((0, 0), (0, unit_count - 2 * high.shape[1]))
    )
    up_all = join_up_near(up_proj[0], after, before, size)
    up_all = join_up_far(up_all, far_up)
    arrived, up_all = lax.optimization_barrier((arrived, up_all))
    shares = exchange(expert_up(arrived, up_all))

    down_all = join_down(down_proj[0], after, before, after_rest, before_rest, far_down, size)
    shares, down_all = lax.optimization_barrier((shares, down_all))
    active = exchange(expert_silu(shares, extra))
    reduced = expert_down(active, down_all, experts, capacity)
    reduced, latent_cache = lax.optimization_barrier((reduced, latent_cache))
    returned = lax.all_to_all(reduced, "dp", split_axis=0, concat_axis=0, tiled=True)
    attended = attention(queries, latent_cache, lengths)
    gate_matrix = gates(active[:, slots:], route, experts, capacity)
    layer_out = combine(gate_matrix, returned, hidden)
    return (attended, layer_out)


def solution(mesh):
    return jax.shard_map(
        on_device,
        mesh=mesh,
        in_specs=(
            P("dp", "hg", None),
            P("dp", "hg", None),
            P("dp"),
            P("dp", None),
            P("hg", "dp", None),
            P(),
            P(None, "hg"),
            P("dp", None),
            P("dp", None, "hg"),
            P("dp", "hg", None),
        ),
        out_specs=(P("dp", "hg", None), P("dp", "hg")),
        check_vma=False,
    )
```

```python
import jax
import jax.numpy as jnp
from jax import lax
from jax.experimental import pallas as pl
from jax.experimental.pallas import tpu as pltpu
from jax.sharding import PartitionSpec as P

LATENT = 512
SOFTMAX_SCALE = 192.0 ** (-0.5)
ROUTE_SCALE = 2.5
NORM_EPS = 1e-06
VMEM_LIMIT = 16 << 20
WHOLE_VMEM = 60 << 20
JOIN_FLOPS = 10 * 10 ** 9
DOWN_FLOPS = 4 * 10 ** 9
ORDER = (0, 1, 3, 2)


def shift(value, distance, size):
    return lax.ppermute(value, "hg", [(i, (i + distance) % size) for i in range(size)])


def spread(value, size):
    return lax.all_to_all(jnp.broadcast_to(value[None], (size,) + value.shape), "hg", 0, 0, tiled=True)


def exchange(value):
    return lax.all_to_all(value, "hg", 0, 0, tiled=True)


def attention(queries, latent_cache, lengths):
    size = lax.axis_size("hg")
    me = lax.axis_index("hg")
    width = latent_cache.shape[1]
    blocks = [latent_cache] + [shift(latent_cache, d, size) for d in range(1, size)]
    whole_cache = jnp.concatenate(blocks, axis=1)
    places = jnp.arange(size * width, dtype=jnp.int32)
    owner = (me - places // width + size) % size
    positions = owner * width + places % width
    scores = (
        jnp.einsum("rhc,rpc->rhp", queries, whole_cache, preferred_element_type=jnp.float32)
        * SOFTMAX_SCALE
    )
    in_range = positions[None, :] < lengths[:, None]
    scores = jnp.where(in_range[:, None, :], scores, -jnp.inf)
    largest = jnp.max(scores, axis=2, keepdims=True)
    weights = jnp.exp(scores - largest)
    probabilities = (weights / jnp.sum(weights, axis=2, keepdims=True)).astype(jnp.bfloat16)
    combined = jnp.einsum(
        "rhp,rpc->rhc",
        probabilities,
        whole_cache[:, :, :LATENT],
        preferred_element_type=jnp.float32,
    )
    return combined.astype(jnp.bfloat16)


HBM = pl.BlockSpec(memory_space=pltpu.HBM)
VMEM = pl.BlockSpec(memory_space=pltpu.VMEM)


def start_all(pairs, sems, first=0):
    copies = [
        pltpu.make_async_copy(source, target, sems.at[first + i])
        for i, (source, target) in enumerate(pairs)
    ]
    for copy in copies:
        copy.start()
    return copies


def wait_all(copies):
    for copy in copies:
        copy.wait()


def place(d, size, width):
    return pl.multiple_of(lax.rem(lax.axis_index("hg") + d, size) * width, 128)


def pack_weights(up_weights, down_weights, earlier, size):
    features, units = up_weights.shape
    part = features // size
    half = units // 2
    chunks = part // 128
    first = chunks // 3
    block = 2 * part
    length = 2 * block + first * units
    assert units == 256 and size == 4 and part % 128 == 0 and block == chunks * units

    def kernel(up_hbm, down_hbm, earlier_ref, next_hbm, back_hbm, up_ref, down_ref, far_ref, next_ref, back_ref, sems):
        def up_block(i, d):
            return up_hbm.at[pl.ds(place(d, size, part), part), :], up_ref.at[i]

        def down_part(i, d):
            return down_hbm.at[:, pl.ds(place(d, size, part), first * 128)], down_ref.at[i]

        far = down_hbm.at[:, pl.ds(place(2, size, part), part)]
        fetched = start_all(
            [up_block(0, 1), up_block(1, 2), down_part(0, 1), up_block(2, 3), (far, far_ref), down_part(1, 3)], sems
        )
        outs = []

        def send(to_ref, to_hbm, at, length):
            piece = slice(at, at + length)
            outs.extend(start_all([(to_ref.at[piece, :], to_hbm.at[piece, :])], sems, 6 + len(outs)))

        for i, to_ref, to_hbm, at in (
            (0, next_ref, next_hbm, 0), (1, next_ref, next_hbm, block), (3, back_ref, back_hbm, 0)
        ):
            fetched[i].wait()
            block_ref = up_ref.at[min(i, 2)]
            to_ref[at:at + part, :] = block_ref[:, :half]
            to_ref[at + part:at + block, :] = block_ref[:, half:]
            send(to_ref, to_hbm, at, block)
            if i == 1:
                fetched[2].wait()
                for k in range(first):
                    to = 2 * block + k * units
                    next_ref[to:to + units, :] = down_ref[0, :, k * 128:(k + 1) * 128]
                send(next_ref, next_hbm, 2 * block, first * units)
        fetched[4].wait()
        for k in range(chunks):
            back_ref[block + k * units:block + (k + 1) * units, :] = far_ref[:, k * 128:(k + 1) * 128]
        send(back_ref, back_hbm, block, block)
        fetched[5].wait()
        for k in range(first):
            to = 2 * block + k * units
            back_ref[to:to + units, :] = down_ref[1, :, k * 128:(k + 1) * 128]
        send(back_ref, back_hbm, 2 * block, first * units)
        wait_all(outs)

    dtype = up_weights.dtype
    return pl.pallas_call(
        kernel,
        out_shape=[pltpu.HBM((length, 128), dtype)] * 2,
        in_specs=[HBM, HBM, pl.BlockSpec(memory_space=pl.ANY)],
        out_specs=[HBM, HBM],
        scratch_shapes=[
            pltpu.VMEM((3, part, units), dtype),
            pltpu.VMEM((2, units, first * 128), dtype),
            pltpu.VMEM((units, part), dtype),
            pltpu.VMEM((length, 128), dtype),
            pltpu.VMEM((length, 128), dtype),
            pltpu.SemaphoreType.DMA((12,)),
        ],
        cost_estimate=pl.CostEstimate(
            flops=0, bytes_accessed=8 * features * units, transcendentals=0
        ),
        compiler_params=pltpu.CompilerParams(vmem_limit_bytes=WHOLE_VMEM),
        name="pack_weights",
    )(up_weights, down_weights, earlier)


def rest_blocks(down_weights, earlier, size):
    units, features = down_weights.shape
    part = features // size
    skip = part // 384 * 128
    width = part - skip

    def kernel(down_hbm, earlier_ref, next_hbm, back_hbm, ref, sems):
        fetched = start_all(
            [
                (down_hbm.at[:, pl.ds(pl.multiple_of(place(d, size, part) + skip, 128), width)], ref.at[i])
                for i, d in enumerate((1, 3))
            ],
            sems,
        )
        outs = []
        for i, out_hbm in enumerate((next_hbm, back_hbm)):
            fetched[i].wait()
            outs += start_all([(ref.at[i], out_hbm)], sems, 2 + i)
        wait_all(outs)

    return pl.pallas_call(
        kernel,
        out_shape=[pltpu.HBM((units, width), down_weights.dtype)] * 2,
        in_specs=[HBM, pl.BlockSpec(memory_space=pl.ANY)],
        out_specs=[HBM, HBM],
        scratch_shapes=[pltpu.VMEM((2, units, width), down_weights.dtype), pltpu.SemaphoreType.DMA((4,))],
        compiler_params=pltpu.CompilerParams(vmem_limit_bytes=WHOLE_VMEM),
        name="rest_blocks",
    )(down_weights, earlier)


def join_up_near(up_weights, after, before, size):
    features, units = up_weights.shape
    part = features // size
    half = units // 2

    def kernel(up_hbm, after_hbm, before_hbm, out_hbm, ref, sems):
        fetched = start_all(
            [(up_hbm.at[pl.ds(place(0, size, part), part), :], ref.at[:, :units])]
            + [
                (hbm.at[j * part:(j + 1) * part, :], ref.at[:, i * units + j * half:i * units + (j + 1) * half])
                for i, hbm in ((1, after_hbm), (2, before_hbm))
                for j in (0, 1)
            ],
            sems,
        )
        wait_all(fetched)
        wait_all(start_all([(ref, out_hbm)], sems, 5))

    dtype = up_weights.dtype
    return pl.pallas_call(
        kernel,
        out_shape=pltpu.HBM((part, 3 * units), dtype),
        in_specs=[HBM] * 3,
        out_specs=HBM,
        scratch_shapes=[pltpu.VMEM((part, 3 * units), dtype), pltpu.SemaphoreType.DMA((6,))],
        cost_estimate=pl.CostEstimate(
            flops=JOIN_FLOPS, bytes_accessed=12 * part * units, transcendentals=0
        ),
        compiler_params=pltpu.CompilerParams(vmem_limit_bytes=WHOLE_VMEM),
        name="join_up_near",
    )(up_weights, after, before)


def join_up_far(joined, far):
    part, width = joined.shape
    half = far.shape[1]

    def kernel(far_ref, joined_hbm, out_ref, sems):
        fetched = start_all([(joined_hbm, out_ref.at[:, :width])], sems)
        out_ref[:, width:width + half] = far_ref[:part, :]
        out_ref[:, width + half:] = far_ref[part:, :]
        wait_all(fetched)

    return pl.pallas_call(
        kernel,
        out_shape=jax.ShapeDtypeStruct((part, width + 2 * half), joined.dtype),
        in_specs=[VMEM, HBM],
        out_specs=VMEM,
        scratch_shapes=[pltpu.SemaphoreType.DMA((1,))],
        compiler_params=pltpu.CompilerParams(vmem_limit_bytes=VMEM_LIMIT),
        name="join_up_far",
    )(far, joined)


def join_down(down_weights, after, before, after_rest, before_rest, far, size):
    units, features = down_weights.shape
    part = features // size
    chunks = part // 128
    first = chunks // 3
    block = 2 * part

    def kernel(
        down_hbm, after_hbm, before_hbm, after_rest_hbm, before_rest_hbm, far_hbm, out_hbm, near_ref, far_ref, ref, sems
    ):
        fetched = start_all(
            [
                (after_hbm.at[2 * block:, :], near_ref.at[0]),
                (before_hbm.at[2 * block:, :], near_ref.at[1]),
                (far_hbm, far_ref),
                (down_hbm.at[:, pl.ds(place(0, size, part), part)], ref.at[:units, :]),
                (after_rest_hbm, ref.at[units:2 * units, first * 128:]),
                (before_rest_hbm, ref.at[2 * units:3 * units, first * 128:]),
            ],
            sems,
        )
        for i in (0, 1):
            fetched[i].wait()
            for k in range(first):
                ref[(i + 1) * units:(i + 2) * units, k * 128:(k + 1) * 128] = near_ref[i, k * units:(k + 1) * units, :]
        fetched[2].wait()
        for k in range(chunks):
            ref[3 * units:, k * 128:(k + 1) * 128] = far_ref[k * units:(k + 1) * units, :]
        wait_all(fetched[3:])
        wait_all(start_all([(ref, out_hbm)], sems, 6))

    dtype = down_weights.dtype
    return pl.pallas_call(
        kernel,
        out_shape=pltpu.HBM((size * units, part), dtype),
        in_specs=[HBM] * 6,
        out_specs=HBM,
        scratch_shapes=[
            pltpu.VMEM((2, first * units, 128), dtype),
            pltpu.VMEM((block, 128), dtype),
            pltpu.VMEM((size * units, part), dtype),
            pltpu.SemaphoreType.DMA((7,)),
        ],
        cost_estimate=pl.CostEstimate(
            flops=DOWN_FLOPS, bytes_accessed=16 * part * units, transcendentals=0
        ),
        compiler_params=pltpu.CompilerParams(vmem_limit_bytes=WHOLE_VMEM),
        name="join_down",
    )(down_weights, after, before, after_rest, before_rest, far)


def norm_and_route(copies, residual, gain, choices, experts, capacity):
    size, rows, features = copies.shape
    part = features // size
    slots = experts * capacity
    top = choices.shape[0]

    def kernel(
        copies_ref, residual_ref, gain_ref, choices_ref, normed_hbm, hidden_hbm, route_hbm, out_hbm,
        hidden_ref, normed_ref, route_ref, out_ref, sems,
    ):
        expert = lax.div(lax.broadcasted_iota(jnp.int32, (slots, rows), 0), capacity)
        slot = lax.broadcasted_iota(jnp.int32, (slots, rows), 0) - expert * capacity
        hits = jnp.zeros((slots, rows), jnp.float32)
        for k in range(top):
            hits += jnp.where(choices_ref[k:k + 1, :] == expert, 1.0, 0.0)
        above = lax.broadcasted_iota(jnp.int32, (rows, rows), 0) < lax.broadcasted_iota(
            jnp.int32, (rows, rows), 1
        )
        earlier = jnp.dot(
            hits.astype(jnp.bfloat16), jnp.where(above, 1.0, 0.0).astype(jnp.bfloat16),
            preferred_element_type=jnp.float32,
        )
        route = jnp.where(earlier == slot.astype(jnp.float32), hits, 0.0).astype(jnp.bfloat16)
        route_ref[...] = route

        hidden = residual_ref[...].astype(jnp.float32)
        for x in range(size):
            hidden += copies_ref[x].astype(jnp.float32)
        hidden_ref[...] = hidden
        scale = lax.rsqrt(jnp.mean(hidden * hidden, axis=1, keepdims=True) + NORM_EPS)
        normed_ref[...] = (hidden * scale * gain_ref[...][None, :]).astype(jnp.bfloat16)
        mine = pl.ds(place(0, size, part), part)
        outs = start_all(
            [(normed_ref, normed_hbm), (hidden_ref.at[:, mine], hidden_hbm), (route_ref, route_hbm)], sems
        )
        out_ref[...] = jnp.dot(
            route, normed_ref[:, mine], preferred_element_type=jnp.float32
        ).astype(jnp.bfloat16).reshape(experts, capacity, part)
        wait_all(outs + start_all([(out_ref, out_hbm)], sems, 3))

    shapes = [
        ((rows, features), jnp.bfloat16),
        ((rows, part), jnp.float32),
        ((slots, rows), jnp.bfloat16),
        ((experts, capacity, part), jnp.bfloat16),
    ]
    return pl.pallas_call(
        kernel,
        out_shape=[pltpu.HBM(*shape) for shape in shapes],
        out_specs=[HBM] * 4,
        scratch_shapes=[
            pltpu.VMEM((rows, features), jnp.float32),
            pltpu.VMEM((rows, features), jnp.bfloat16),
            pltpu.VMEM((slots, rows), jnp.bfloat16),
            pltpu.VMEM((experts, capacity, part), jnp.bfloat16),
            pltpu.SemaphoreType.DMA((4,)),
        ],
        cost_estimate=pl.CostEstimate(
            flops=2 * slots * rows * part,
            bytes_accessed=2 * (size + 2) * rows * features + 2 * slots * part,
            transcendentals=0,
        ),
        compiler_params=pltpu.CompilerParams(vmem_limit_bytes=VMEM_LIMIT),
        name="norm_and_route",
    )(copies, residual, gain, choices)


def gates(logit_parts, route, experts, capacity):
    size, rows, lanes = logit_parts.shape
    slots = experts * capacity
    local = experts // size

    def kernel(parts_ref, route_ref, out_ref):
        expert = lax.div(lax.broadcasted_iota(jnp.int32, (slots, lanes), 0), capacity)
        lane = lax.broadcasted_iota(jnp.int32, (slots, lanes), 1)
        column = jnp.where(lane < local, lane, lane - local)
        logits = jnp.zeros((slots, rows), jnp.float32)
        for x in range(size):
            pick = (column + x * local == expert) & (lane < 2 * local)
            logits += lax.dot_general(
                jnp.where(pick, 1.0, 0.0).astype(jnp.bfloat16), parts_ref[x],
                (((1,), (1,)), ((), ())), preferred_element_type=jnp.float32,
            )
        affinity = route_ref[...].astype(jnp.float32) / (1.0 + jnp.exp(-logits))
        total = jnp.sum(affinity, axis=0, keepdims=True)
        out_ref[...] = (ROUTE_SCALE * affinity / total).astype(jnp.bfloat16)

    return pl.pallas_call(
        kernel,
        out_shape=jax.ShapeDtypeStruct((slots, rows), jnp.bfloat16),
        name="gates",
    )(logit_parts, route)


def combine(gate_matrix, returned, hidden):
    experts, capacity, part = returned.shape
    slots = experts * capacity

    def kernel(gates_hbm, returned_ref, hidden_hbm, out_ref, gates_ref, hidden_ref, sems):
        copies = start_all([(gates_hbm, gates_ref), (hidden_hbm, hidden_ref)], sems)
        wait_all(copies)
        routed = lax.dot_general(
            gates_ref[...], returned_ref[...].reshape(slots, part), (((0,), (0,)), ((), ())),
            preferred_element_type=jnp.float32,
        )
        out_ref[...] = (hidden_ref[...] + routed).astype(jnp.bfloat16)

    return pl.pallas_call(
        kernel,
        out_shape=jax.ShapeDtypeStruct(hidden.shape, jnp.bfloat16),
        in_specs=[HBM, VMEM, HBM],
        scratch_shapes=[
            pltpu.VMEM(gate_matrix.shape, gate_matrix.dtype),
            pltpu.VMEM(hidden.shape, hidden.dtype),
            pltpu.SemaphoreType.DMA((2,)),
        ],
        compiler_params=pltpu.CompilerParams(vmem_limit_bytes=VMEM_LIMIT),
        name="combine",
    )(gate_matrix, returned, hidden)


def expert_up(arrived, weights):
    size = lax.axis_size("hg")
    experts, capacity, part = arrived.shape
    slots = experts * capacity
    units = weights.shape[1] // size

    def kernel(rows_ref, weights_ref, out_hbm, out_ref, sems):
        me = lax.axis_index("hg")
        rows = rows_ref[...].reshape(slots, part)
        outs = []
        for i, d in enumerate(ORDER):
            out_ref[i] = jnp.dot(
                rows, weights_ref[:, i * units:(i + 1) * units],
                preferred_element_type=jnp.float32,
            ).astype(jnp.bfloat16)
            outs += start_all([(out_ref.at[i], out_hbm.at[lax.rem(me + size - d, size)])], sems, i)
        wait_all(outs)

    return pl.pallas_call(
        kernel,
        out_shape=pltpu.HBM((size, slots, units), jnp.bfloat16),
        in_specs=[VMEM, VMEM],
        out_specs=HBM,
        scratch_shapes=[
            pltpu.VMEM((size, slots, units), jnp.bfloat16), pltpu.SemaphoreType.DMA((size,))
        ],
        cost_estimate=pl.CostEstimate(
            flops=2 * slots * size * part * units,
            bytes_accessed=2 * (slots * part + size * part * units + size * slots * units),
            transcendentals=0,
        ),
        compiler_params=pltpu.CompilerParams(vmem_limit_bytes=VMEM_LIMIT),
        name="expert_up",
    )(arrived, weights)


def expert_silu(shares, extra):
    size, slots, units = shares.shape
    more = extra.shape[0]

    def kernel(shares_ref, extra_hbm, out_hbm, active_ref, sems):
        copies = start_all([(extra_hbm, active_ref.at[slots:, :])], sems)
        total = shares_ref[0].astype(jnp.float32)
        for x in range(1, size):
            total += shares_ref[x].astype(jnp.float32)
        active_ref[:slots, :] = (total / (1.0 + jnp.exp(-total))).astype(jnp.bfloat16)
        wait_all(copies)
        wait_all(start_all([(active_ref, out_hbm.at[x]) for x in range(size)], sems, 1))

    return pl.pallas_call(
        kernel,
        out_shape=pltpu.HBM((size, slots + more, units), jnp.bfloat16),
        in_specs=[VMEM, pl.BlockSpec(memory_space=pl.ANY)],
        out_specs=HBM,
        scratch_shapes=[
            pltpu.VMEM((slots + more, units), jnp.bfloat16),
            pltpu.SemaphoreType.DMA((size + 1,)),
        ],
        cost_estimate=pl.CostEstimate(
            flops=8 * slots * units,
            bytes_accessed=4 * size * slots * units,
            transcendentals=slots * units,
        ),
        compiler_params=pltpu.CompilerParams(vmem_limit_bytes=VMEM_LIMIT),
        name="expert_silu",
    )(shares, extra)


def expert_down(active, weights, experts, capacity):
    size, _, units = active.shape
    part = weights.shape[1]
    slots = experts * capacity

    cut = experts // 2

    def kernel(active_ref, weights_ref, out_hbm, out_ref, sems):
        me = lax.axis_index("hg")
        outs = []
        for half in (0, 1):
            rows = slice(half * cut * capacity, (half + 1) * cut * capacity)
            total = jnp.zeros((cut * capacity, part), jnp.float32)
            for i, d in enumerate(ORDER):
                total += jnp.dot(
                    active_ref[lax.rem(me + size - d, size), rows, :],
                    weights_ref[i * units:(i + 1) * units, :],
                    preferred_element_type=jnp.float32,
                )
            some = slice(half * cut, (half + 1) * cut)
            out_ref[some] = total.astype(jnp.bfloat16).reshape(cut, capacity, part)
            outs += start_all([(out_ref.at[some], out_hbm.at[some])], sems, half)
        wait_all(outs)

    return pl.pallas_call(
        kernel,
        out_shape=pltpu.HBM((experts, capacity, part), jnp.bfloat16),
        in_specs=[VMEM, VMEM],
        out_specs=HBM,
        scratch_shapes=[
            pltpu.VMEM((experts, capacity, part), jnp.bfloat16), pltpu.SemaphoreType.DMA((2,))
        ],
        cost_estimate=pl.CostEstimate(
            flops=2 * slots * size * part * units,
            bytes_accessed=2 * (slots * size * units + size * part * units + slots * part),
            transcendentals=0,
        ),
        compiler_params=pltpu.CompilerParams(vmem_limit_bytes=VMEM_LIMIT),
        name="expert_down",
    )(active, weights)


def on_device(
    queries,
    latent_cache,
    lengths,
    residual,
    partials,
    norm_gain,
    router,
    expert_ids,
    up_proj,
    down_proj,
):
    size = lax.axis_size("hg")
    row_count, feature_width = residual.shape
    top_count = expert_ids.shape[1]
    experts = lax.axis_size("dp") * up_proj.shape[0]
    capacity = min(row_count, max(2, 2 * row_count * top_count // experts))
    unit_count = up_proj.shape[2]
    slots = experts * capacity

    copies = jnp.broadcast_to(partials[0][None], (size,) + partials.shape[1:])
    to_next, to_back = pack_weights(up_proj[0], down_proj[0], copies, size)
    after, before = shift(to_next, 1, size), shift(to_back, size - 1, size)
    block = 2 * (feature_width // size)
    far_up = shift(after[block:2 * block], 1, size)
    far_down = shift(before[block:2 * block], size - 1, size)
    normed, hidden, route, outgoing = norm_and_route(
        exchange(copies), residual, norm_gain, expert_ids.T, experts, capacity
    )
    next_rest, back_rest = rest_blocks(down_proj[0], normed, size)
    next_rest, back_rest, before = lax.optimization_barrier((next_rest, back_rest, before))
    after_rest, before_rest = shift(next_rest, 1, size), shift(back_rest, size - 1, size)
    arrived = lax.all_to_all(outgoing, "dp", split_axis=0, concat_axis=0, tiled=True)

    local_logits = jnp.dot(normed, router, preferred_element_type=jnp.float32)
    high = local_logits.astype(jnp.bfloat16)
    low = (local_logits - high.astype(jnp.float32)).astype(jnp.bfloat16)
    extra = jnp.pad(
        jnp.concatenate([high, low], axis=1), ((0, 0), (0, unit_count - 2 * high.shape[1]))
    )
    up_all = join_up_near(up_proj[0], after, before, size)
    up_all = join_up_far(up_all, far_up)
    arrived, up_all = lax.optimization_barrier((arrived, up_all))
    shares = exchange(expert_up(arrived, up_all))

    down_all = join_down(down_proj[0], after, before, after_rest, before_rest, far_down, size)
    shares, down_all = lax.optimization_barrier((shares, down_all))
    active = exchange(expert_silu(shares, extra))
    reduced = expert_down(active, down_all, experts, capacity)
    reduced, latent_cache = lax.optimization_barrier((reduced, latent_cache))
    returned = lax.all_to_all(reduced, "dp", split_axis=0, concat_axis=0, tiled=True)
    attended = attention(queries, latent_cache, lengths)
    gate_matrix = gates(active[:, slots:], route, experts, capacity)
    layer_out = combine(gate_matrix, returned, hidden)
    return (attended, layer_out)


def solution(mesh):
    return jax.shard_map(
        on_device,
        mesh=mesh,
        in_specs=(
            P("dp", "hg", None),
            P("dp", "hg", None),
            P("dp"),
            P("dp", None),
            P("hg", "dp", None),
            P(),
            P(None, "hg"),
            P("dp", None),
            P("dp", None, "hg"),
            P("dp", "hg", None),
        ),
        out_specs=(P("dp", "hg", None), P("dp", "hg")),
        check_vma=False,
    )
```

```python
import jax
import jax.numpy as jnp
from jax import lax
from jax.experimental import pallas as pl
from jax.experimental.pallas import tpu as pltpu
from jax.sharding import PartitionSpec as P

LATENT = 512
SOFTMAX_SCALE = 192.0 ** (-0.5)
ROUTE_SCALE = 2.5
NORM_EPS = 1e-06
VMEM_LIMIT = 16 << 20
WHOLE_VMEM = 60 << 20
JOIN_FLOPS = 8 * 10 ** 9
DOWN_FLOPS = 4 * 10 ** 9
ORDER = (0, 1, 3, 2)


def shift(value, distance, size):
    return lax.ppermute(value, "hg", [(i, (i + distance) % size) for i in range(size)])


def spread(value, size):
    return lax.all_to_all(jnp.broadcast_to(value[None], (size,) + value.shape), "hg", 0, 0, tiled=True)


def exchange(value):
    return lax.all_to_all(value, "hg", 0, 0, tiled=True)


def attention(queries, latent_cache, lengths):
    size = lax.axis_size("hg")
    me = lax.axis_index("hg")
    width = latent_cache.shape[1]
    blocks = [latent_cache] + [shift(latent_cache, d, size) for d in range(1, size)]
    whole_cache = jnp.concatenate(blocks, axis=1)
    places = jnp.arange(size * width, dtype=jnp.int32)
    owner = (me - places // width + size) % size
    positions = owner * width + places % width
    scores = (
        jnp.einsum("rhc,rpc->rhp", queries, whole_cache, preferred_element_type=jnp.float32)
        * SOFTMAX_SCALE
    )
    in_range = positions[None, :] < lengths[:, None]
    scores = jnp.where(in_range[:, None, :], scores, -jnp.inf)
    largest = jnp.max(scores, axis=2, keepdims=True)
    weights = jnp.exp(scores - largest)
    probabilities = (weights / jnp.sum(weights, axis=2, keepdims=True)).astype(jnp.bfloat16)
    combined = jnp.einsum(
        "rhp,rpc->rhc",
        probabilities,
        whole_cache[:, :, :LATENT],
        preferred_element_type=jnp.float32,
    )
    return combined.astype(jnp.bfloat16)


HBM = pl.BlockSpec(memory_space=pltpu.HBM)
VMEM = pl.BlockSpec(memory_space=pltpu.VMEM)


def start_all(pairs, sems, first=0):
    copies = [
        pltpu.make_async_copy(source, target, sems.at[first + i])
        for i, (source, target) in enumerate(pairs)
    ]
    for copy in copies:
        copy.start()
    return copies


def wait_all(copies):
    for copy in copies:
        copy.wait()


def place(d, size, width):
    return pl.multiple_of(lax.rem(lax.axis_index("hg") + d, size) * width, 128)


def pack_weights(up_weights, down_weights, earlier, size):
    features, units = up_weights.shape
    part = features // size
    half = units // 2
    chunks = part // 128
    first = chunks // 3
    block = 2 * part
    length = 2 * block + first * units
    assert units == 256 and size == 4 and part % 128 == 0 and block == chunks * units

    def kernel(up_hbm, down_hbm, earlier_ref, next_hbm, back_hbm, up_ref, down_ref, far_ref, next_ref, back_ref, sems):
        def up_block(i, d):
            return up_hbm.at[pl.ds(place(d, size, part), part), :], up_ref.at[i]

        def down_part(i, d):
            return down_hbm.at[:, pl.ds(place(d, size, part), first * 128)], down_ref.at[i]

        far = down_hbm.at[:, pl.ds(place(2, size, part), part)]
        fetched = start_all(
            [up_block(0, 1), up_block(1, 2), down_part(0, 1), up_block(2, 3), (far, far_ref), down_part(1, 3)], sems
        )
        outs = []

        def send(to_ref, to_hbm, at, length):
            piece = slice(at, at + length)
            outs.extend(start_all([(to_ref.at[piece, :], to_hbm.at[piece, :])], sems, 6 + len(outs)))

        for i, to_ref, to_hbm, at in (
            (0, next_ref, next_hbm, 0), (1, next_ref, next_hbm, block), (3, back_ref, back_hbm, 0)
        ):
            fetched[i].wait()
            block_ref = up_ref.at[min(i, 2)]
            to_ref[at:at + part, :] = block_ref[:, :half]
            to_ref[at + part:at + block, :] = block_ref[:, half:]
            send(to_ref, to_hbm, at, block)
            if i == 1:
                fetched[2].wait()
                for k in range(first):
                    to = 2 * block + k * units
                    next_ref[to:to + units, :] = down_ref[0, :, k * 128:(k + 1) * 128]
                send(next_ref, next_hbm, 2 * block, first * units)
        fetched[4].wait()
        for k in range(chunks):
            back_ref[block + k * units:block + (k + 1) * units, :] = far_ref[:, k * 128:(k + 1) * 128]
        send(back_ref, back_hbm, block, block)
        fetched[5].wait()
        for k in range(first):
            to = 2 * block + k * units
            back_ref[to:to + units, :] = down_ref[1, :, k * 128:(k + 1) * 128]
        send(back_ref, back_hbm, 2 * block, first * units)
        wait_all(outs)

    dtype = up_weights.dtype
    return pl.pallas_call(
        kernel,
        out_shape=[pltpu.HBM((length, 128), dtype)] * 2,
        in_specs=[HBM, HBM, pl.BlockSpec(memory_space=pl.ANY)],
        out_specs=[HBM, HBM],
        scratch_shapes=[
            pltpu.VMEM((3, part, units), dtype),
            pltpu.VMEM((2, units, first * 128), dtype),
            pltpu.VMEM((units, part), dtype),
            pltpu.VMEM((length, 128), dtype),
            pltpu.VMEM((length, 128), dtype),
            pltpu.SemaphoreType.DMA((12,)),
        ],
        cost_estimate=pl.CostEstimate(
            flops=0, bytes_accessed=8 * features * units, transcendentals=0
        ),
        compiler_params=pltpu.CompilerParams(vmem_limit_bytes=WHOLE_VMEM),
        name="pack_weights",
    )(up_weights, down_weights, earlier)


def rest_blocks(down_weights, earlier, size):
    units, features = down_weights.shape
    part = features // size
    skip = part // 384 * 128
    width = part - skip

    def kernel(down_hbm, earlier_ref, next_hbm, back_hbm, ref, sems):
        fetched = start_all(
            [
                (down_hbm.at[:, pl.ds(pl.multiple_of(place(d, size, part) + skip, 128), width)], ref.at[i])
                for i, d in enumerate((1, 3))
            ],
            sems,
        )
        outs = []
        for i, out_hbm in enumerate((next_hbm, back_hbm)):
            fetched[i].wait()
            outs += start_all([(ref.at[i], out_hbm)], sems, 2 + i)
        wait_all(outs)

    return pl.pallas_call(
        kernel,
        out_shape=[pltpu.HBM((units, width), down_weights.dtype)] * 2,
        in_specs=[HBM, pl.BlockSpec(memory_space=pl.ANY)],
        out_specs=[HBM, HBM],
        scratch_shapes=[pltpu.VMEM((2, units, width), down_weights.dtype), pltpu.SemaphoreType.DMA((4,))],
        compiler_params=pltpu.CompilerParams(vmem_limit_bytes=WHOLE_VMEM),
        name="rest_blocks",
    )(down_weights, earlier)


def join_up_near(up_weights, after, before, size):
    features, units = up_weights.shape
    part = features // size
    half = units // 2

    def kernel(up_hbm, after_hbm, before_hbm, out_hbm, ref, sems):
        fetched = start_all(
            [(up_hbm.at[pl.ds(place(0, size, part), part), :], ref.at[:, :units])]
            + [
                (hbm.at[j * part:(j + 1) * part, :], ref.at[:, i * units + j * half:i * units + (j + 1) * half])
                for i, hbm in ((1, after_hbm), (2, before_hbm))
                for j in (0, 1)
            ],
            sems,
        )
        wait_all(fetched)
        wait_all(start_all([(ref, out_hbm)], sems, 5))

    dtype = up_weights.dtype
    return pl.pallas_call(
        kernel,
        out_shape=pltpu.HBM((part, 3 * units), dtype),
        in_specs=[HBM] * 3,
        out_specs=HBM,
        scratch_shapes=[pltpu.VMEM((part, 3 * units), dtype), pltpu.SemaphoreType.DMA((6,))],
        cost_estimate=pl.CostEstimate(
            flops=JOIN_FLOPS, bytes_accessed=12 * part * units, transcendentals=0
        ),
        compiler_params=pltpu.CompilerParams(vmem_limit_bytes=WHOLE_VMEM),
        name="join_up_near",
    )(up_weights, after, before)


def join_up_far(joined, far):
    part, width = joined.shape
    half = far.shape[1]

    def kernel(far_ref, joined_hbm, out_ref, sems):
        fetched = start_all([(joined_hbm, out_ref.at[:, :width])], sems)
        out_ref[:, width:width + half] = far_ref[:part, :]
        out_ref[:, width + half:] = far_ref[part:, :]
        wait_all(fetched)

    return pl.pallas_call(
        kernel,
        out_shape=jax.ShapeDtypeStruct((part, width + 2 * half), joined.dtype),
        in_specs=[VMEM, HBM],
        out_specs=VMEM,
        scratch_shapes=[pltpu.SemaphoreType.DMA((1,))],
        compiler_params=pltpu.CompilerParams(vmem_limit_bytes=VMEM_LIMIT),
        name="join_up_far",
    )(far, joined)


def join_down(down_weights, after, before, after_rest, before_rest, far, size):
    units, features = down_weights.shape
    part = features // size
    chunks = part // 128
    first = chunks // 3
    block = 2 * part

    def kernel(
        down_hbm, after_hbm, before_hbm, after_rest_hbm, before_rest_hbm, far_hbm, out_hbm, near_ref, far_ref, ref, sems
    ):
        fetched = start_all(
            [
                (after_hbm.at[2 * block:, :], near_ref.at[0]),
                (before_hbm.at[2 * block:, :], near_ref.at[1]),
                (far_hbm, far_ref),
                (down_hbm.at[:, pl.ds(place(0, size, part), part)], ref.at[:units, :]),
                (after_rest_hbm, ref.at[units:2 * units, first * 128:]),
                (before_rest_hbm, ref.at[2 * units:3 * units, first * 128:]),
            ],
            sems,
        )
        for i in (0, 1):
            fetched[i].wait()
            for k in range(first):
                ref[(i + 1) * units:(i + 2) * units, k * 128:(k + 1) * 128] = near_ref[i, k * units:(k + 1) * units, :]
        fetched[2].wait()
        for k in range(chunks):
            ref[3 * units:, k * 128:(k + 1) * 128] = far_ref[k * units:(k + 1) * units, :]
        wait_all(fetched[3:])
        wait_all(start_all([(ref, out_hbm)], sems, 6))

    dtype = down_weights.dtype
    return pl.pallas_call(
        kernel,
        out_shape=pltpu.HBM((size * units, part), dtype),
        in_specs=[HBM] * 6,
        out_specs=HBM,
        scratch_shapes=[
            pltpu.VMEM((2, first * units, 128), dtype),
            pltpu.VMEM((block, 128), dtype),
            pltpu.VMEM((size * units, part), dtype),
            pltpu.SemaphoreType.DMA((7,)),
        ],
        cost_estimate=pl.CostEstimate(
            flops=DOWN_FLOPS, bytes_accessed=16 * part * units, transcendentals=0
        ),
        compiler_params=pltpu.CompilerParams(vmem_limit_bytes=WHOLE_VMEM),
        name="join_down",
    )(down_weights, after, before, after_rest, before_rest, far)


def norm_and_route(copies, residual, gain, choices, experts, capacity):
    size, rows, features = copies.shape
    part = features // size
    slots = experts * capacity
    top = choices.shape[0]

    def kernel(
        copies_ref, residual_ref, gain_ref, choices_ref, normed_hbm, hidden_hbm, route_hbm, out_hbm,
        hidden_ref, normed_ref, route_ref, out_ref, sems,
    ):
        expert = lax.div(lax.broadcasted_iota(jnp.int32, (slots, rows), 0), capacity)
        slot = lax.broadcasted_iota(jnp.int32, (slots, rows), 0) - expert * capacity
        hits = jnp.zeros((slots, rows), jnp.float32)
        for k in range(top):
            hits += jnp.where(choices_ref[k:k + 1, :] == expert, 1.0, 0.0)
        above = lax.broadcasted_iota(jnp.int32, (rows, rows), 0) < lax.broadcasted_iota(
            jnp.int32, (rows, rows), 1
        )
        earlier = jnp.dot(
            hits.astype(jnp.bfloat16), jnp.where(above, 1.0, 0.0).astype(jnp.bfloat16),
            preferred_element_type=jnp.float32,
        )
        route = jnp.where(earlier == slot.astype(jnp.float32), hits, 0.0).astype(jnp.bfloat16)
        route_ref[...] = route

        hidden = residual_ref[...].astype(jnp.float32)
        for x in range(size):
            hidden += copies_ref[x].astype(jnp.float32)
        hidden_ref[...] = hidden
        scale = lax.rsqrt(jnp.mean(hidden * hidden, axis=1, keepdims=True) + NORM_EPS)
        normed_ref[...] = (hidden * scale * gain_ref[...][None, :]).astype(jnp.bfloat16)
        mine = pl.ds(place(0, size, part), part)
        outs = start_all(
            [(normed_ref, normed_hbm), (hidden_ref.at[:, mine], hidden_hbm), (route_ref, route_hbm)], sems
        )
        out_ref[...] = jnp.dot(
            route, normed_ref[:, mine], preferred_element_type=jnp.float32
        ).astype(jnp.bfloat16).reshape(experts, capacity, part)
        wait_all(outs + start_all([(out_ref, out_hbm)], sems, 3))

    shapes = [
        ((rows, features), jnp.bfloat16),
        ((rows, part), jnp.float32),
        ((slots, rows), jnp.bfloat16),
        ((experts, capacity, part), jnp.bfloat16),
    ]
    return pl.pallas_call(
        kernel,
        out_shape=[pltpu.HBM(*shape) for shape in shapes],
        out_specs=[HBM] * 4,
        scratch_shapes=[
            pltpu.VMEM((rows, features), jnp.float32),
            pltpu.VMEM((rows, features), jnp.bfloat16),
            pltpu.VMEM((slots, rows), jnp.bfloat16),
            pltpu.VMEM((experts, capacity, part), jnp.bfloat16),
            pltpu.SemaphoreType.DMA((4,)),
        ],
        cost_estimate=pl.CostEstimate(
            flops=2 * slots * rows * part,
            bytes_accessed=2 * (size + 2) * rows * features + 2 * slots * part,
            transcendentals=0,
        ),
        compiler_params=pltpu.CompilerParams(vmem_limit_bytes=VMEM_LIMIT),
        name="norm_and_route",
    )(copies, residual, gain, choices)


def gates(logit_parts, route, experts, capacity):
    size, rows, lanes = logit_parts.shape
    slots = experts * capacity
    local = experts // size

    def kernel(parts_ref, route_ref, out_ref):
        expert = lax.div(lax.broadcasted_iota(jnp.int32, (slots, lanes), 0), capacity)
        lane = lax.broadcasted_iota(jnp.int32, (slots, lanes), 1)
        column = jnp.where(lane < local, lane, lane - local)
        logits = jnp.zeros((slots, rows), jnp.float32)
        for x in range(size):
            pick = (column + x * local == expert) & (lane < 2 * local)
            logits += lax.dot_general(
                jnp.where(pick, 1.0, 0.0).astype(jnp.bfloat16), parts_ref[x],
                (((1,), (1,)), ((), ())), preferred_element_type=jnp.float32,
            )
        affinity = route_ref[...].astype(jnp.float32) / (1.0 + jnp.exp(-logits))
        total = jnp.sum(affinity, axis=0, keepdims=True)
        out_ref[...] = (ROUTE_SCALE * affinity / total).astype(jnp.bfloat16)

    return pl.pallas_call(
        kernel,
        out_shape=jax.ShapeDtypeStruct((slots, rows), jnp.bfloat16),
        name="gates",
    )(logit_parts, route)


def combine(gate_matrix, returned, hidden):
    experts, capacity, part = returned.shape
    slots = experts * capacity

    def kernel(gates_hbm, returned_ref, hidden_hbm, out_ref, gates_ref, hidden_ref, sems):
        copies = start_all([(gates_hbm, gates_ref), (hidden_hbm, hidden_ref)], sems)
        wait_all(copies)
        routed = lax.dot_general(
            gates_ref[...], returned_ref[...].reshape(slots, part), (((0,), (0,)), ((), ())),
            preferred_element_type=jnp.float32,
        )
        out_ref[...] = (hidden_ref[...] + routed).astype(jnp.bfloat16)

    return pl.pallas_call(
        kernel,
        out_shape=jax.ShapeDtypeStruct(hidden.shape, jnp.bfloat16),
        in_specs=[HBM, VMEM, HBM],
        scratch_shapes=[
            pltpu.VMEM(gate_matrix.shape, gate_matrix.dtype),
            pltpu.VMEM(hidden.shape, hidden.dtype),
            pltpu.SemaphoreType.DMA((2,)),
        ],
        compiler_params=pltpu.CompilerParams(vmem_limit_bytes=VMEM_LIMIT),
        name="combine",
    )(gate_matrix, returned, hidden)


def expert_up(arrived, weights):
    size = lax.axis_size("hg")
    experts, capacity, part = arrived.shape
    slots = experts * capacity
    units = weights.shape[1] // size

    def kernel(rows_ref, weights_ref, out_hbm, out_ref, sems):
        me = lax.axis_index("hg")
        rows = rows_ref[...].reshape(slots, part)
        outs = []
        for i, d in enumerate(ORDER):
            out_ref[i] = jnp.dot(
                rows, weights_ref[:, i * units:(i + 1) * units],
                preferred_element_type=jnp.float32,
            ).astype(jnp.bfloat16)
            outs += start_all([(out_ref.at[i], out_hbm.at[lax.rem(me + size - d, size)])], sems, i)
        wait_all(outs)

    return pl.pallas_call(
        kernel,
        out_shape=pltpu.HBM((size, slots, units), jnp.bfloat16),
        in_specs=[VMEM, VMEM],
        out_specs=HBM,
        scratch_shapes=[
            pltpu.VMEM((size, slots, units), jnp.bfloat16), pltpu.SemaphoreType.DMA((size,))
        ],
        cost_estimate=pl.CostEstimate(
            flops=2 * slots * size * part * units,
            bytes_accessed=2 * (slots * part + size * part * units + size * slots * units),
            transcendentals=0,
        ),
        compiler_params=pltpu.CompilerParams(vmem_limit_bytes=VMEM_LIMIT),
        name="expert_up",
    )(arrived, weights)


def expert_silu(shares, extra):
    size, slots, units = shares.shape
    more = extra.shape[0]

    def kernel(shares_ref, extra_hbm, out_hbm, active_ref, sems):
        copies = start_all([(extra_hbm, active_ref.at[slots:, :])], sems)
        total = shares_ref[0].astype(jnp.float32)
        for x in range(1, size):
            total += shares_ref[x].astype(jnp.float32)
        active_ref[:slots, :] = (total / (1.0 + jnp.exp(-total))).astype(jnp.bfloat16)
        wait_all(copies)
        wait_all(start_all([(active_ref, out_hbm.at[x]) for x in range(size)], sems, 1))

    return pl.pallas_call(
        kernel,
        out_shape=pltpu.HBM((size, slots + more, units), jnp.bfloat16),
        in_specs=[VMEM, pl.BlockSpec(memory_space=pl.ANY)],
        out_specs=HBM,
        scratch_shapes=[
            pltpu.VMEM((slots + more, units), jnp.bfloat16),
            pltpu.SemaphoreType.DMA((size + 1,)),
        ],
        cost_estimate=pl.CostEstimate(
            flops=8 * slots * units,
            bytes_accessed=4 * size * slots * units,
            transcendentals=slots * units,
        ),
        compiler_params=pltpu.CompilerParams(vmem_limit_bytes=VMEM_LIMIT),
        name="expert_silu",
    )(shares, extra)


def expert_down(active, weights, experts, capacity):
    size, _, units = active.shape
    part = weights.shape[1]
    slots = experts * capacity

    cut = experts // 2

    def kernel(active_ref, weights_ref, out_hbm, out_ref, sems):
        me = lax.axis_index("hg")
        outs = []
        for half in (0, 1):
            rows = slice(half * cut * capacity, (half + 1) * cut * capacity)
            total = jnp.zeros((cut * capacity, part), jnp.float32)
            for i, d in enumerate(ORDER):
                total += jnp.dot(
                    active_ref[lax.rem(me + size - d, size), rows, :],
                    weights_ref[i * units:(i + 1) * units, :],
                    preferred_element_type=jnp.float32,
                )
            some = slice(half * cut, (half + 1) * cut)
            out_ref[some] = total.astype(jnp.bfloat16).reshape(cut, capacity, part)
            outs += start_all([(out_ref.at[some], out_hbm.at[some])], sems, half)
        wait_all(outs)

    return pl.pallas_call(
        kernel,
        out_shape=pltpu.HBM((experts, capacity, part), jnp.bfloat16),
        in_specs=[VMEM, VMEM],
        out_specs=HBM,
        scratch_shapes=[
            pltpu.VMEM((experts, capacity, part), jnp.bfloat16), pltpu.SemaphoreType.DMA((2,))
        ],
        cost_estimate=pl.CostEstimate(
            flops=2 * slots * size * part * units,
            bytes_accessed=2 * (slots * size * units + size * part * units + slots * part),
            transcendentals=0,
        ),
        compiler_params=pltpu.CompilerParams(vmem_limit_bytes=VMEM_LIMIT),
        name="expert_down",
    )(active, weights)


def on_device(
    queries,
    latent_cache,
    lengths,
    residual,
    partials,
    norm_gain,
    router,
    expert_ids,
    up_proj,
    down_proj,
):
    size = lax.axis_size("hg")
    row_count, feature_width = residual.shape
    top_count = expert_ids.shape[1]
    experts = lax.axis_size("dp") * up_proj.shape[0]
    capacity = min(row_count, max(2, 2 * row_count * top_count // experts))
    unit_count = up_proj.shape[2]
    slots = experts * capacity

    copies = jnp.broadcast_to(partials[0][None], (size,) + partials.shape[1:])
    to_next, to_back = pack_weights(up_proj[0], down_proj[0], copies, size)
    after, before = shift(to_next, 1, size), shift(to_back, size - 1, size)
    block = 2 * (feature_width // size)
    far_up = shift(after[block:2 * block], 1, size)
    far_down = shift(before[block:2 * block], size - 1, size)
    normed, hidden, route, outgoing = norm_and_route(
        exchange(copies), residual, norm_gain, expert_ids.T, experts, capacity
    )
    next_rest, back_rest = rest_blocks(down_proj[0], normed, size)
    up_all = join_up_near(up_proj[0], after, before, size)
    next_rest, back_rest, up_all = lax.optimization_barrier((next_rest, back_rest, up_all))
    after_rest, before_rest = shift(next_rest, 1, size), shift(back_rest, size - 1, size)
    arrived = lax.all_to_all(outgoing, "dp", split_axis=0, concat_axis=0, tiled=True)

    local_logits = jnp.dot(normed, router, preferred_element_type=jnp.float32)
    high = local_logits.astype(jnp.bfloat16)
    low = (local_logits - high.astype(jnp.float32)).astype(jnp.bfloat16)
    extra = jnp.pad(
        jnp.concatenate([high, low], axis=1), ((0, 0), (0, unit_count - 2 * high.shape[1]))
    )
    up_all = join_up_far(up_all, far_up)
    arrived, up_all = lax.optimization_barrier((arrived, up_all))
    shares = exchange(expert_up(arrived, up_all))

    down_all = join_down(down_proj[0], after, before, after_rest, before_rest, far_down, size)
    shares, down_all = lax.optimization_barrier((shares, down_all))
    active = exchange(expert_silu(shares, extra))
    reduced = expert_down(active, down_all, experts, capacity)
    reduced, latent_cache = lax.optimization_barrier((reduced, latent_cache))
    returned = lax.all_to_all(reduced, "dp", split_axis=0, concat_axis=0, tiled=True)
    attended = attention(queries, latent_cache, lengths)
    gate_matrix = gates(active[:, slots:], route, experts, capacity)
    layer_out = combine(gate_matrix, returned, hidden)
    return (attended, layer_out)


def solution(mesh):
    return jax.shard_map(
        on_device,
        mesh=mesh,
        in_specs=(
            P("dp", "hg", None),
            P("dp", "hg", None),
            P("dp"),
            P("dp", None),
            P("hg", "dp", None),
            P(),
            P(None, "hg"),
            P("dp", None),
            P("dp", None, "hg"),
            P("dp", "hg", None),
        ),
        out_specs=(P("dp", "hg", None), P("dp", "hg")),
        check_vma=False,
    )
```
